32 devices in a mesh: energy: 8 (over y, x, core), domain: 4 (over z).
Axes of the slice: x: 2, y: 2, z: 4, core: 2. Of those that a mesh axis runs over, the one named last changes fastest.
Arguments:
- inverses: bfloat16 [16, 4, 2, 416, 416], P('energy', 'domain'), may hold values from -6 to 6
- coupling: bfloat16 [4, 416, 416], P('domain'), may hold values from -0.015625 to 0.015625
- lead_green: bfloat16 [16, 2, 416, 416], P('energy'), may hold values from -6 to 6
- phonon: bfloat16 [16, 4, 2, 6656], P('energy', 'domain'), may hold values from -0.0024414062 to 0.0024414062
- neighbors: int32 [4, 416, 16], P('domain'), may hold values from 0 to 415
- shifts: int32 [16], replicated, may hold values from -4 to 4
Outputs:
- green_out: bfloat16 [16, 4, 2, 416, 416], P('energy', 'domain')
The draws below stay inside these ranges and needn't reach their ends.
Inputs may be any that keep to these rules, and one draw needn't show every extreme that they name: `neighbors`: each entry is an orbital of the same block; an orbital may stand more than once in a row.
All inputs are finite; a program needn't handle non-finite values.
Results may differ from the reference program's by a relative error of at most 0.025.
Values may be sent and summed in bfloat16 or wider, within the bound.
No kernel may reach another device: no remote copies, remote signals or barrier semaphores. Data moves between devices by JAX's collectives and lax.ppermute only.
A program may use at most 128 MiB of HBM per device.

```python
import jax
import jax.numpy as jnp
from jax import lax

O = 416
K = 16
NE = 16
NBLK = 4
PAIRS = 6656
SHIFT_MAX = 4


def draw_shifts(key, part):
    key = jax.random.fold_in(key, 11)
    shuffled = jax.random.permutation(key, NE)
    return (shuffled % (2 * SHIFT_MAX + 1) - SHIFT_MAX).astype(jnp.int32)


def touch_ends(entries, key, smallest, largest):
    longest = entries.shape.index(max(entries.shape))
    spots = []
    for shift in (0, 1):
        where = [jax.random.randint(jax.random.fold_in(key, axis), (), 0, length) for axis, length in enumerate(entries.shape)]
        where[longest] = (where[longest] + shift) % entries.shape[longest]
        spots.append(tuple(where))
    return entries.at[spots[0]].set(smallest).at[spots[1]].set(largest)


def levels(own_key, shape, shards, least, high):
    factor_of, own = 1.0, jax.random.fold_in(own_key, 6)
    for dim, blocks in shards:
        steps = jnp.exp(jax.random.uniform(jax.random.fold_in(own, dim), (blocks,), jnp.float32, least / len(shards), high / len(shards)))
        factor_of = factor_of * jnp.repeat(steps, shape[dim] // blocks).reshape([-1 if axis == dim else 1 for axis in range(len(shape))])
    return factor_of


def normal_values(stream_key, extent, spread, reach, shards=(), held_as=jnp.bfloat16):
    values = spread * jax.random.normal(stream_key, extent, jnp.float32)
    if shards:
        values = values * levels(stream_key, extent, shards, -0.22, 0.18)
    return jnp.clip(values, -reach, reach).astype(held_as)


def setup_inputs(seed: int = 0) -> dict:
    key_of = jax.random.split(jax.random.key(seed), 7)
    return {
        "inverses": normal_values(key_of[0], (NE, NBLK, 2, O, O), 1.0, 6.0, ((0, 8), (1, 4))),
        "coupling": normal_values(key_of[1], (NBLK, O, O), (O * O) ** -0.5, 0.015625, ((0, 4),)),
        "lead_green": normal_values(key_of[2], (NE, 2, O, O), 1.0, 6.0, ((0, 8),)),
        "phonon": normal_values(key_of[3], (NE, NBLK, 2, PAIRS), (64 * O * K * NE) ** -0.5, 0.0024414062, ((0, 8), (1, 4))),
        "neighbors": touch_ends(jax.random.randint(key_of[4], (NBLK, O, K), 0, O), jax.random.fold_in(key_of[4], 1), 0, O - 1).astype(jnp.int32),
        "shifts": draw_shifts(jax.random.fold_in(key_of[6], 71), 0),
    }


precise = lax.Precision.HIGHEST


def rounded(array):
    return lax.optimization_barrier(array.astype(jnp.bfloat16))


def complex_times(first_factor, second_factor):
    first_wide = first_factor.astype(jnp.float32)
    second_wide = second_factor.astype(jnp.float32)
    real_part = jnp.einsum("bij,bjk->bik", first_wide[:, 0], second_wide[:, 0], precision=precise) - jnp.einsum("bij,bjk->bik", first_wide[:, 1], second_wide[:, 1], precision=precise)
    imag_part = jnp.einsum("bij,bjk->bik", first_wide[:, 0], second_wide[:, 1], precision=precise) + jnp.einsum("bij,bjk->bik", first_wide[:, 1], second_wide[:, 0], precision=precise)
    return jnp.stack([real_part, imag_part], axis=1)


def reference(inverses, coupling, lead_green, phonon, neighbors, shifts):
    coupling_wide = coupling.astype(jnp.float32)
    coupling_next = jnp.concatenate([coupling_wide[1:], jnp.zeros((1, O, O), jnp.float32)], axis=0)

    def green_of_energy(operands):
        inverse_row, lead_row = operands
        inverse_wide = inverse_row.astype(jnp.float32)
        previous = jnp.concatenate([lead_row.astype(jnp.float32)[None], inverse_wide[:-1]], axis=0)
        following = jnp.concatenate([inverse_wide[1:], jnp.zeros((1, 2, O, O), jnp.float32)], axis=0)
        left_product = rounded(jnp.einsum("bcij,bjk->bcik", previous, coupling_wide, precision=precise))
        left_self = rounded(jnp.einsum("bji,bcjk->bcik", coupling_wide, left_product.astype(jnp.float32), precision=precise))
        right_product = rounded(jnp.einsum("bcij,bkj->bcik", following, coupling_next, precision=precise))
        right_self = rounded(jnp.einsum("bij,bcjk->bcik", coupling_next, right_product.astype(jnp.float32), precision=precise))
        coupled = rounded(left_self.astype(jnp.float32) + right_self.astype(jnp.float32))
        inner_term = rounded(complex_times(coupled, inverse_row))
        return (inverse_wide + complex_times(inverse_row, inner_term)).astype(jnp.bfloat16)

    green_blocks = lax.map(green_of_energy, (inverses, lead_green))
    columns = jnp.broadcast_to(neighbors[None, :, None], (NE, NBLK, 2, O, K))
    pair_green = jnp.take_along_axis(green_blocks, columns, axis=4).reshape(NE, NBLK, 2, PAIRS).astype(jnp.float32)
    points = jnp.arange(NE, dtype=jnp.int32)
    samples = phonon.astype(jnp.float32)

    def convolve(running, operands):
        sample_row, offset = operands
        source = points - offset
        inside = ((source >= 0) & (source < NE)).astype(jnp.float32)
        taken = jnp.take(pair_green, jnp.clip(source, 0, NE - 1), axis=0) * inside[:, None, None, None]
        real_part = sample_row[:, 0] * taken[:, :, 0] - sample_row[:, 1] * taken[:, :, 1]
        imag_part = sample_row[:, 0] * taken[:, :, 1] + sample_row[:, 1] * taken[:, :, 0]
        return running + jnp.stack([real_part, imag_part], axis=2), None

    self_sum = lax.scan(convolve, jnp.zeros((NE, NBLK, 2, PAIRS), jnp.float32), (samples, shifts))[0]
    self_pairs = rounded(self_sum)
    block_index = jnp.arange(NBLK, dtype=jnp.int32)[:, None, None, None]
    part_index = jnp.arange(2, dtype=jnp.int32)[None, :, None, None]
    row_index = jnp.arange(O, dtype=jnp.int32)[None, None, :, None]
    column_index = neighbors[:, None, :, :]

    def dyson_of_energy(operands):
        green_row, pair_row = operands
        values = pair_row.astype(jnp.float32).reshape(NBLK, 2, O, K)
        self_block = rounded(jnp.zeros((NBLK, 2, O, O), jnp.float32).at[block_index, part_index, row_index, column_index].add(values))
        scattered = rounded(complex_times(green_row, self_block))
        return (green_row.astype(jnp.float32) + complex_times(scattered, green_row)).astype(jnp.bfloat16)

    return lax.map(dyson_of_energy, (green_blocks, self_pairs))
```

```python
import functools

import jax
import jax.numpy as jnp
from jax import lax
from jax.experimental import pallas as pl
from jax.experimental.pallas import tpu as pltpu
from jax.sharding import PartitionSpec as P

LANES = 128
SUBLANES = 8
VMEM_LIMIT = 48 * 1024 * 1024


def product(first, second):
    return jnp.dot(first, second, preferred_element_type=jnp.float32)


def product_nt(first, second):
    return lax.dot_general(
        first, second, (((1,), (1,)), ((), ())), preferred_element_type=jnp.float32
    )


def product_tn(first, second):
    return lax.dot_general(
        first, second, (((0,), (0,)), ((), ())), preferred_element_type=jnp.float32
    )


def packed_rows(orbitals):
    return 2 * orbitals * orbitals // LANES


def pack_planes(out_ref, planes):
    orbitals = planes[0].shape[0]
    whole = orbitals // LANES
    rest = orbitals - whole * LANES
    pieces = LANES // rest // 2
    height = orbitals // pieces
    for c, plane in enumerate(planes):
        for t in range(whole):
            out_ref[pl.ds((c * whole + t) * orbitals, orbitals), :] = plane[
                :, t * LANES : (t + 1) * LANES
            ]
    tails = [
        plane[h * height : (h + 1) * height, whole * LANES :]
        for plane in planes
        for h in range(pieces)
    ]
    out_ref[pl.ds(2 * whole * orbitals, height), :] = jnp.concatenate(tails, axis=1)


def unpack_planes(packed_ref, plane_ref):
    orbitals = plane_ref.shape[1]
    whole = orbitals // LANES
    rest = orbitals - whole * LANES
    pieces = LANES // rest // 2
    height = orbitals // pieces
    tails = packed_ref[pl.ds(2 * whole * orbitals, height), :]
    for c in range(2):
        for t in range(whole):
            plane_ref[c, :, t * LANES : (t + 1) * LANES] = packed_ref[
                pl.ds((c * whole + t) * orbitals, orbitals), :
            ]
        for h in range(pieces):
            start = (c * pieces + h) * rest
            plane_ref[c, h * height : (h + 1) * height, whole * LANES :] = tails[
                :, start : start + rest
            ]


def pack_kernel(e, inverse_ref, up_ref):
    pack_planes(up_ref, [inverse_ref[e, 0, 0], inverse_ref[e, 0, 1]])


def right_kernel(e, inverse_ref, coupling_ref, down_ref):
    coupling = coupling_ref[0]
    planes = []
    for c in range(2):
        right_product = product_nt(inverse_ref[e, 0, c], coupling).astype(jnp.bfloat16)
        planes.append(product(coupling, right_product).astype(jnp.bfloat16))
    pack_planes(down_ref, planes)


def group_iotas():
    sublane = lax.broadcasted_iota(jnp.int32, (SUBLANES, LANES), 0)
    lane = lax.broadcasted_iota(jnp.int32, (SUBLANES, LANES), 1)
    return sublane, lane


def along_lanes(values, lanes):
    return jnp.take_along_axis(values, lanes, axis=1, mode="promise_in_bounds")


def table_kernel(width, neighbors_ref, phonon_ref, columns_ref, slots_ref, same_ref, phonon_out_ref, wide, flat, samples):
    orbitals = neighbors_ref.shape[1]
    groups = orbitals // SUBLANES
    sublane, lane = group_iotas()
    own = sublane == lane // width
    wide[...] = jnp.zeros(wide.shape, wide.dtype)
    wide[:, :width] = neighbors_ref[0]
    flat[...] = jnp.full(flat.shape, -1.0, flat.dtype)
    tiles = slots_ref.shape[1] // LANES
    for r in range(groups):
        rows = slice(r * SUBLANES, (r + 1) * SUBLANES)
        group = wide[rows, :]
        columns = along_lanes(group, lane % width)
        columns_ref[rows, :] = columns
        flat[r : r + 1, :] = jnp.sum(
            jnp.where(own, columns.astype(jnp.float32), 0.0), axis=0, keepdims=True
        )
        found = [jnp.full((SUBLANES, LANES), -1, jnp.int32) for _ in range(tiles)]
        for k in range(width):
            column = jnp.broadcast_to(group[:, k : k + 1], (SUBLANES, LANES))
            slot = sublane * width + k
            for t in range(tiles):
                found[t] = jnp.where(column == lane + t * LANES, slot, found[t])
        for t in range(tiles):
            slots_ref[rows, t * LANES : (t + 1) * LANES] = found[t]
    for d in range(1, width):
        turned = (lane // width) * width + (lane + d) % width
        for r in range(flat.shape[0] // SUBLANES):
            rows = slice(r * SUBLANES, (r + 1) * SUBLANES)
            here = flat[rows, :]
            there = along_lanes(here, turned)
            same_ref[d - 1, rows, :] = jnp.where(here == there, 1.0, 0.0)
    samples[...] = jnp.zeros(samples.shape, samples.dtype)
    for e in range(phonon_ref.shape[0]):
        for r in range(groups):
            samples[e, :, r, :] = phonon_ref[e, 0, :, r * LANES : (r + 1) * LANES].astype(
                jnp.float32
            )
    phonon_out_ref[...] = samples[...].astype(jnp.bfloat16)


def green_kernel(
    e, width, up_ref, down_ref, lead_ref, inverse_ref, coupling_ref, columns_ref,
    green_ref, pair_ref, previous, right_self, wide, flat,
):
    orbitals = inverse_ref.shape[3]
    at_start = lax.axis_index("domain") == 0

    @pl.when(at_start)
    def _():
        previous[...] = lead_ref[e]

    @pl.when(jnp.logical_not(at_start))
    def _():
        unpack_planes(up_ref, previous)

    unpack_planes(down_ref, right_self)
    coupling = coupling_ref[0]
    inverse = [inverse_ref[e, 0, c] for c in range(2)]
    coupled = []
    for c in range(2):
        left_product = product(previous[c], coupling).astype(jnp.bfloat16)
        left_self = product_tn(coupling, left_product).astype(jnp.bfloat16)
        coupled.append(
            (left_self.astype(jnp.float32) + right_self[c].astype(jnp.float32)).astype(jnp.bfloat16)
        )
    inner_real = (product(coupled[0], inverse[0]) - product(coupled[1], inverse[1])).astype(jnp.bfloat16)
    inner_imag = (product(coupled[0], inverse[1]) + product(coupled[1], inverse[0])).astype(jnp.bfloat16)
    real = product(inverse[0], inner_real) - product(inverse[1], inner_imag)
    imag = product(inverse[0], inner_imag) + product(inverse[1], inner_real)
    for c, part in enumerate((real, imag)):
        green = (inverse[c].astype(jnp.float32) + part).astype(jnp.bfloat16)
        green_ref[c] = green
        wide[c, :, :orbitals] = green.astype(jnp.float32)
    gather_pairs(width, wide, columns_ref, flat, pair_ref)


def gather_pairs(width, wide, columns_ref, flat, pair_ref):
    orbitals = columns_ref.shape[0]
    tiles = wide.shape[2] // LANES
    sublane, lane = group_iotas()
    own = sublane == lane // width
    flat[...] = jnp.zeros(flat.shape, flat.dtype)
    for r in range(orbitals // SUBLANES):
        rows = slice(r * SUBLANES, (r + 1) * SUBLANES)
        columns = columns_ref[rows, :]
        within = columns & (LANES - 1)
        tile = columns // LANES
        for c in range(2):
            taken = jnp.zeros((SUBLANES, LANES), jnp.float32)
            for t in range(tiles):
                candidate = along_lanes(wide[c, rows, t * LANES : (t + 1) * LANES], within)
                taken = jnp.where(own & (tile == t), candidate, taken)
            flat[c, r : r + 1, :] = jnp.sum(taken, axis=0, keepdims=True)
    pair_ref[0] = flat[...].astype(jnp.bfloat16)


def final_kernel(
    width, shifts_ref, phonon_ref, even_ref, odd_ref, slots_ref, same_ref, green_even_ref, green_odd_ref,
    out_ref, merged, self_block,
):
    points = phonon_ref.shape[0]
    orbitals = out_ref.shape[3]
    height = phonon_ref.shape[2]
    groups = orbitals // SUBLANES
    tiles = slots_ref.shape[1] // LANES
    me = lax.axis_index("energy")
    _, lane = group_iotas()
    for e, green_ref in enumerate((green_even_ref, green_odd_ref)):

        def add_point(w, sums):
            source = 2 * me + e - shifts_ref[w]
            inside = (source >= 0) & (source < points)
            source = jnp.clip(source, 0, points - 1)
            owner = source // 2
            keep = jnp.where(inside, 1.0, 0.0)
            odd = source - 2 * owner == 1
            sample = [phonon_ref[w, c].astype(jnp.float32) * keep for c in range(2)]
            taken = [
                jnp.where(odd, odd_ref[owner, c], even_ref[owner, c]).astype(jnp.float32)
                for c in range(2)
            ]
            return (
                sums[0] + (sample[0] * taken[0] - sample[1] * taken[1]),
                sums[1] + (sample[0] * taken[1] + sample[1] * taken[0]),
            )

        zero = jnp.zeros((height, LANES), jnp.float32)
        sums = lax.fori_loop(0, points, add_point, (zero, zero))
        for c in range(2):
            pairs = sums[c].astype(jnp.bfloat16).astype(jnp.float32)
            for r in range(height // SUBLANES):
                rows = slice(r * SUBLANES, (r + 1) * SUBLANES)
                group = pairs[rows]
                total = group
                for d in range(1, width):
                    turned = (lane // width) * width + (lane + d) % width
                    total = total + same_ref[d - 1, rows, :] * along_lanes(group, turned)
                merged[c, rows, :] = total
        for q in range(groups // 2):
            for t in range(tiles):
                found = [[], []]
                for r in (2 * q, 2 * q + 1):
                    slot = slots_ref[r * SUBLANES : (r + 1) * SUBLANES, t * LANES : (t + 1) * LANES]
                    within = slot & (LANES - 1)
                    for c in range(2):
                        row = jnp.broadcast_to(merged[c, r : r + 1, :], (SUBLANES, LANES))
                        found[c].append(jnp.where(slot >= 0, along_lanes(row, within), 0.0))
                for c in range(2):
                    self_block[c, q * 16 : (q + 1) * 16, t * LANES : (t + 1) * LANES] = (
                        jnp.concatenate(found[c], axis=0).astype(jnp.bfloat16)
                    )
        green = [green_ref[c] for c in range(2)]
        sigma = [self_block[c, :, :orbitals] for c in range(2)]
        real = (product(green[0], sigma[0]) - product(green[1], sigma[1])).astype(jnp.bfloat16)
        imag = (product(green[0], sigma[1]) + product(green[1], sigma[0])).astype(jnp.bfloat16)
        out_ref[e, 0, 0] = (
            green[0].astype(jnp.float32) + (product(real, green[0]) - product(imag, green[1]))
        ).astype(jnp.bfloat16)
        out_ref[e, 0, 1] = (
            green[1].astype(jnp.float32) + (product(real, green[1]) + product(imag, green[0]))
        ).astype(jnp.bfloat16)


IN_VMEM = pl.BlockSpec(memory_space=pltpu.VMEM)
IN_SMEM = pl.BlockSpec(memory_space=pltpu.SMEM)


def call(kernel, out_shape, in_specs, scratch=(), flops=0, bytes_accessed=1 << 20):
    return pl.pallas_call(
        kernel,
        out_shape=out_shape,
        in_specs=in_specs,
        out_specs=jax.tree.map(lambda s: IN_VMEM, out_shape),
        scratch_shapes=list(scratch),
        compiler_params=pltpu.CompilerParams(vmem_limit_bytes=VMEM_LIMIT),
        cost_estimate=pl.CostEstimate(flops=flops, bytes_accessed=bytes_accessed, transcendentals=0),
    )


def body(inverses, coupling, lead_green, phonon, neighbors, shifts):
    energies = inverses.shape[0]
    orbitals = inverses.shape[3]
    width = neighbors.shape[2]
    points = shifts.shape[0]
    rows = packed_rows(orbitals)
    groups = orbitals * width // LANES
    height = -(-groups // 16) * 16
    padded = -(-orbitals // LANES) * LANES
    bf16, f32 = jnp.bfloat16, jnp.float32
    shape = jax.ShapeDtypeStruct
    cube = 2 * orbitals**3
    ends = lax.axis_size("domain") - 1
    upward = [(i, i + 1) for i in range(ends)]
    downward = [(i + 1, i) for i in range(ends)]

    from_below, from_above = [], []
    for e in range(energies):
        up = call(functools.partial(pack_kernel, e), shape((rows, LANES), bf16), [IN_VMEM])(inverses)
        from_below.append(lax.ppermute(up, "domain", upward))
        down = call(
            functools.partial(right_kernel, e),
            shape((rows, LANES), bf16),
            [IN_VMEM] * 2,
            flops=4 * cube,
        )(inverses, coupling)
        from_above.append(lax.ppermute(down, "domain", downward))

    columns, slots, same, samples = call(
        functools.partial(table_kernel, width),
        (
            shape((orbitals, LANES), jnp.int32),
            shape((orbitals, padded), jnp.int32),
            shape((width - 1, height, LANES), f32),
            shape((energies, 2, height, LANES), bf16),
        ),
        [IN_VMEM] * 2,
        [
            pltpu.VMEM((orbitals, LANES), jnp.int32),
            pltpu.VMEM((height, LANES), f32),
            pltpu.VMEM((energies, 2, height, LANES), f32),
        ],
    )(neighbors, phonon)
    phonon_all = lax.all_gather(samples, "energy", axis=0, tiled=True)

    greens, pairs = [], []
    for e in range(energies):
        green, pair = call(
            functools.partial(green_kernel, e, width),
            (shape((2, orbitals, orbitals), bf16), shape((1, 2, height, LANES), bf16)),
            [IN_VMEM] * 6,
            [
                pltpu.VMEM((2, orbitals, orbitals), bf16),
                pltpu.VMEM((2, orbitals, orbitals), bf16),
                pltpu.VMEM((2, orbitals, padded), f32),
                pltpu.VMEM((2, height, LANES), f32),
            ],
            flops=12 * cube,
        )(from_below[e], from_above[e], lead_green, inverses, coupling, columns)
        greens.append(green)
        pairs.append(lax.all_gather(pair, "energy", axis=0, tiled=True))

    return call(
        functools.partial(final_kernel, width),
        shape((energies, 1, 2, orbitals, orbitals), bf16),
        [IN_SMEM] + [IN_VMEM] * 7,
        [
            pltpu.VMEM((2, height, LANES), f32),
            pltpu.VMEM((2, orbitals, padded), bf16),
        ],
        flops=16 * cube,
    )(shifts, phonon_all, pairs[0], pairs[1], slots, same, greens[0], greens[1])


def solution(mesh):
    return jax.shard_map(
        body,
        mesh=mesh,
        in_specs=(
            P("energy", "domain", None, None, None),
            P("domain", None, None),
            P("energy", None, None, None),
            P("energy", "domain", None, None),
            P("domain", None, None),
            P(),
        ),
        out_specs=P("energy", "domain", None, None, None),
        check_vma=False,
    )
```

```python
import functools

import jax
import jax.numpy as jnp
from jax import lax
from jax.experimental import pallas as pl
from jax.experimental.pallas import tpu as pltpu
from jax.sharding import PartitionSpec as P

LANES = 128
SUBLANES = 8
MIB = 1024 * 1024


def product(first, second):
    return jnp.dot(first, second, preferred_element_type=jnp.float32)


def product_nt(first, second):
    return lax.dot_general(
        first, second, (((1,), (1,)), ((), ())), preferred_element_type=jnp.float32
    )


def product_tn(first, second):
    return lax.dot_general(
        first, second, (((0,), (0,)), ((), ())), preferred_element_type=jnp.float32
    )


def packed_rows(orbitals):
    return 2 * orbitals * orbitals // LANES


def pack_planes(out_ref, planes):
    orbitals = planes[0].shape[0]
    whole = orbitals // LANES
    rest = orbitals - whole * LANES
    pieces = LANES // rest // 2
    height = orbitals // pieces
    for c, plane in enumerate(planes):
        for t in range(whole):
            out_ref[pl.ds((c * whole + t) * orbitals, orbitals), :] = plane[
                :, t * LANES : (t + 1) * LANES
            ]
    tails = [
        plane[h * height : (h + 1) * height, whole * LANES :]
        for plane in planes
        for h in range(pieces)
    ]
    out_ref[pl.ds(2 * whole * orbitals, height), :] = jnp.concatenate(tails, axis=1)


def unpack_planes(packed_ref, plane_ref):
    orbitals = plane_ref.shape[1]
    whole = orbitals // LANES
    rest = orbitals - whole * LANES
    pieces = LANES // rest // 2
    height = orbitals // pieces
    tails = packed_ref[pl.ds(2 * whole * orbitals, height), :]
    for c in range(2):
        for t in range(whole):
            plane_ref[c, :, t * LANES : (t + 1) * LANES] = packed_ref[
                pl.ds((c * whole + t) * orbitals, orbitals), :
            ]
        for h in range(pieces):
            start = (c * pieces + h) * rest
            plane_ref[c, h * height : (h + 1) * height, whole * LANES :] = tails[
                :, start : start + rest
            ]


def send_kernel(e, inverses_ref, coupling_ref, up_ref, down_ref, inverse, coupling, sems):
    copies = [pltpu.make_async_copy(coupling_ref.at[0], coupling, sems.at[2])]
    for c in range(2):
        copies.append(pltpu.make_async_copy(inverses_ref.at[e, 0, c], inverse.at[c], sems.at[c]))
    for copy in copies:
        copy.start()
    copies[0].wait()
    planes = []
    for c in range(2):
        copies[1 + c].wait()
        right_product = product_nt(inverse[c], coupling[...]).astype(jnp.bfloat16)
        planes.append(product(coupling[...], right_product).astype(jnp.bfloat16))
    pack_planes(down_ref, planes)
    pack_planes(up_ref, [inverse[c] for c in range(2)])


def group_iotas():
    sublane = lax.broadcasted_iota(jnp.int32, (SUBLANES, LANES), 0)
    lane = lax.broadcasted_iota(jnp.int32, (SUBLANES, LANES), 1)
    return sublane, lane


def along_lanes(values, lanes):
    return jnp.take_along_axis(values, lanes, axis=1, mode="promise_in_bounds")


def table_kernel(
    width, neighbors_ref, phonon_ref, lead_ref, inverses_ref, coupling_ref,
    columns_ref, slots_ref, samples_ref, lead_held, inverses_held, coupling_held,
    wide, flat, samples, sems,
):
    fetches = [
        pltpu.make_async_copy(source, held, sems.at[i])
        for i, (source, held) in enumerate(
            ((coupling_ref, coupling_held), (inverses_ref, inverses_held), (lead_ref, lead_held))
        )
    ]
    for fetch in fetches:
        fetch.start()
    orbitals = neighbors_ref.shape[1]
    groups = orbitals // SUBLANES
    energies = phonon_ref.shape[0]
    sublane, lane = group_iotas()
    own = sublane == lane // width
    wide[...] = jnp.zeros(wide.shape, wide.dtype)
    wide[:, :width] = neighbors_ref[0]
    flat[...] = jnp.full(flat.shape, -1.0, flat.dtype)
    samples[...] = jnp.zeros(samples.shape, samples.dtype)
    tiles = slots_ref.shape[1] // LANES
    for r in range(groups):
        rows = slice(r * SUBLANES, (r + 1) * SUBLANES)
        group = wide[rows, :]
        columns = along_lanes(group, lane % width)
        columns_ref[rows, :] = columns
        flat[r : r + 1, :] = jnp.sum(
            jnp.where(own, columns.astype(jnp.float32), 0.0), axis=0, keepdims=True
        )
        found = [jnp.full((SUBLANES, LANES), -1, jnp.int32) for _ in range(tiles)]
        for k in range(width):
            column = jnp.broadcast_to(group[:, k : k + 1], (SUBLANES, LANES))
            slot = sublane * width + k
            for t in range(tiles):
                found[t] = jnp.where(column == lane + t * LANES, slot, found[t])
        for t in range(tiles):
            slots_ref[rows, t * LANES : (t + 1) * LANES] = found[t]
        for e in range(energies):
            samples[e, :, r, :] = phonon_ref[e, 0, :, r * LANES : (r + 1) * LANES].astype(
                jnp.float32
            )
    for r in range(flat.shape[0] // SUBLANES):
        rows = slice(r * SUBLANES, (r + 1) * SUBLANES)
        here = flat[rows, :]
        values = [[samples[e, c, rows, :] for c in range(2)] for e in range(energies)]
        totals = [list(pair) for pair in values]
        for d in range(1, width):
            turned = (lane // width) * width + (lane + d) % width
            same = here == along_lanes(here, turned)
            for e in range(energies):
                for c in range(2):
                    totals[e][c] = totals[e][c] + jnp.where(
                        same, along_lanes(values[e][c], turned), 0.0
                    )
        for e in range(energies):
            for c in range(2):
                samples[e, c, rows, :] = totals[e][c]
    samples_ref[...] = samples[...].astype(jnp.bfloat16)
    for fetch in fetches:
        fetch.wait()


def unpack_kernel(packed_ref, plane_ref):
    unpack_planes(packed_ref, plane_ref)


def green_kernel(
    e, width, up_ref, right_self, lead_ref, inverses_ref, coupling_ref, columns_ref, *rest
):
    *pair_before, green_ref, pair_ref, previous, wide, flat = rest
    orbitals = inverses_ref.shape[3]
    at_start = lax.axis_index("domain") == 0

    @pl.when(at_start)
    def _():
        previous[...] = lead_ref[e]

    @pl.when(jnp.logical_not(at_start))
    def _():
        unpack_planes(up_ref, previous)

    coupling = coupling_ref[0]
    inverse = [inverses_ref[e, 0, c] for c in range(2)]
    coupled = []
    for c in range(2):
        left_product = product(previous[c], coupling).astype(jnp.bfloat16)
        left_self = product_tn(coupling, left_product).astype(jnp.bfloat16)
        coupled.append(
            (left_self.astype(jnp.float32) + right_self[c].astype(jnp.float32)).astype(jnp.bfloat16)
        )
    inner_real = (product(coupled[0], inverse[0]) - product(coupled[1], inverse[1])).astype(jnp.bfloat16)
    inner_imag = (product(coupled[0], inverse[1]) + product(coupled[1], inverse[0])).astype(jnp.bfloat16)
    real = product(inverse[0], inner_real) - product(inverse[1], inner_imag)
    imag = product(inverse[0], inner_imag) + product(inverse[1], inner_real)
    for c, part in enumerate((real, imag)):
        green = (inverse[c].astype(jnp.float32) + part).astype(jnp.bfloat16)
        green_ref[c] = green
        wide[c, :, :orbitals] = green.astype(jnp.float32)
    for k, ref in enumerate(pair_before):
        pair_ref[k] = ref[0]
    gather_pairs(width, wide, columns_ref, flat, pair_ref, len(pair_before))


def gather_pairs(width, wide, columns_ref, flat, pair_ref, place):
    orbitals = columns_ref.shape[0]
    tiles = wide.shape[2] // LANES
    sublane, lane = group_iotas()
    own = sublane == lane // width
    flat[...] = jnp.zeros(flat.shape, flat.dtype)
    for r in range(orbitals // SUBLANES):
        rows = slice(r * SUBLANES, (r + 1) * SUBLANES)
        columns = columns_ref[rows, :]
        within = columns & (LANES - 1)
        tile = columns // LANES
        for c in range(2):
            taken = jnp.zeros((SUBLANES, LANES), jnp.float32)
            for t in range(tiles):
                candidate = along_lanes(wide[c, rows, t * LANES : (t + 1) * LANES], within)
                taken = jnp.where(own & (tile == t), candidate, taken)
            flat[c, r : r + 1, :] = jnp.sum(taken, axis=0, keepdims=True)
    pair_ref[place] = flat[...].astype(jnp.bfloat16)


def final_kernel(
    shifts_ref, samples_ref, pairs_ref, slots_ref, green_even_ref, green_odd_ref,
    out_ref, sources, merged, self_block, result, sems,
):
    points = shifts_ref.shape[0]
    orbitals = result.shape[2]
    groups = orbitals // SUBLANES
    tiles = slots_ref.shape[1] // LANES
    used = merged.shape[2]
    me = lax.axis_index("energy")

    def widen(p, _):
        for c in range(2):
            sources[p, c] = pairs_ref[p, c].astype(jnp.float32)
        return _

    lax.fori_loop(0, points, widen, 0, unroll=4)

    def add_point(w, sums):
        shift = shifts_ref[w]
        sample = [samples_ref[w, c].astype(jnp.float32)[:used] for c in range(2)]
        after = []
        for e in range(2):
            source = 2 * me + e - shift
            keep = jnp.where((source >= 0) & (source < points), 1.0, 0.0)
            source = jnp.clip(source, 0, points - 1)
            real, imag = (sources[source, c, :used, :] for c in range(2))
            after.append(
                (
                    sums[e][0] + keep * (sample[0] * real - sample[1] * imag),
                    sums[e][1] + keep * (sample[0] * imag + sample[1] * real),
                )
            )
        return tuple(after)

    zero = jnp.zeros((used, LANES), jnp.float32)
    sums = lax.fori_loop(0, points, add_point, ((zero, zero), (zero, zero)), unroll=4)
    for e in range(2):
        for c in range(2):
            merged[e, c] = sums[e][c]
    copies = []
    for e, green_ref in enumerate((green_even_ref, green_odd_ref)):
        for q in range(groups // 2):
            for t in range(tiles):
                found = [[], []]
                for r in (2 * q, 2 * q + 1):
                    slot = slots_ref[r * SUBLANES : (r + 1) * SUBLANES, t * LANES : (t + 1) * LANES]
                    within = slot & (LANES - 1)
                    for c in range(2):
                        row = jnp.broadcast_to(merged[e, c, r : r + 1, :], (SUBLANES, LANES))
                        found[c].append(jnp.where(slot >= 0, along_lanes(row, within), 0.0))
                for c in range(2):
                    self_block[e, c, q * 16 : (q + 1) * 16, t * LANES : (t + 1) * LANES] = (
                        jnp.concatenate(found[c], axis=0).astype(jnp.bfloat16)
                    )
    for e, green_ref in enumerate((green_even_ref, green_odd_ref)):
        green = [green_ref[c] for c in range(2)]
        sigma = [self_block[e, c, :, :orbitals] for c in range(2)]
        real = (product(green[0], sigma[0]) - product(green[1], sigma[1])).astype(jnp.bfloat16)
        imag = (product(green[0], sigma[1]) + product(green[1], sigma[0])).astype(jnp.bfloat16)
        result[e, 0] = (
            green[0].astype(jnp.float32) + (product(real, green[0]) - product(imag, green[1]))
        ).astype(jnp.bfloat16)
        copies.append(pltpu.make_async_copy(result.at[e, 0], out_ref.at[e, 0, 0], sems.at[e, 0]))
        copies[-1].start()
        result[e, 1] = (
            green[1].astype(jnp.float32) + (product(real, green[1]) + product(imag, green[0]))
        ).astype(jnp.bfloat16)
        copies.append(pltpu.make_async_copy(result.at[e, 1], out_ref.at[e, 0, 1], sems.at[e, 1]))
        copies[-1].start()
    for copy in copies:
        copy.wait()


IN_VMEM = pl.BlockSpec(memory_space=pltpu.VMEM)
IN_SMEM = pl.BlockSpec(memory_space=pltpu.SMEM)
IN_HBM = pl.BlockSpec(memory_space=pltpu.HBM)


def call(kernel, out_shape, in_specs, scratch=(), flops=0, bytes_accessed=1 << 20, out_spec=None, limit=4):
    return pl.pallas_call(
        kernel,
        out_shape=out_shape,
        in_specs=in_specs,
        out_specs=out_spec or (IN_VMEM if not isinstance(out_shape, tuple) else (IN_VMEM,) * len(out_shape)),
        scratch_shapes=list(scratch),
        compiler_params=pltpu.CompilerParams(vmem_limit_bytes=limit * MIB),
        cost_estimate=pl.CostEstimate(flops=flops, bytes_accessed=bytes_accessed, transcendentals=0),
    )


def body(inverses, coupling, lead_green, phonon, neighbors, shifts):
    energies = inverses.shape[0]
    orbitals = inverses.shape[3]
    width = neighbors.shape[2]
    rows = packed_rows(orbitals)
    groups = orbitals * width // LANES
    used = -(-groups // SUBLANES) * SUBLANES
    height = -(-groups // 16) * 16
    padded = -(-orbitals // LANES) * LANES
    bf16, f32 = jnp.bfloat16, jnp.float32
    shape = jax.ShapeDtypeStruct
    cube = 2 * orbitals**3
    plane = (orbitals, orbitals)
    ends = lax.axis_size("domain") - 1
    upward = [(i, i + 1) for i in range(ends)]
    downward = [(i + 1, i) for i in range(ends)]

    from_below, from_above = [], []

    in_hbm = [
        pltpu.with_memory_space_constraint(array, pltpu.HBM)
        for array in (inverses, coupling, lead_green)
    ]

    barred = in_hbm[0]
    for e in range(energies):
        up, down = call(
            functools.partial(send_kernel, e),
            (shape((rows, LANES), bf16), shape((rows, LANES), bf16)),
            [IN_HBM] * 2,
            [
                pltpu.VMEM((2, *plane), bf16),
                pltpu.VMEM(plane, bf16),
                pltpu.SemaphoreType.DMA((3,)),
            ],
            flops=4 * cube,
        )(barred, in_hbm[1])
        from_above.append(lax.ppermute(down, "domain", downward))
        from_below.append(lax.ppermute(up, "domain", upward))
        barred, neighbors, _ = lax.optimization_barrier((barred, neighbors, down))
        barred = pltpu.with_memory_space_constraint(barred, pltpu.HBM)
    columns, slots, samples, lead, inverses, coupling = call(
        functools.partial(table_kernel, width),
        (
            shape((orbitals, LANES), jnp.int32),
            shape((orbitals, padded), jnp.int32),
            shape((energies, 2, height, LANES), bf16),
            pltpu.VMEM(lead_green.shape, bf16),
            pltpu.VMEM(inverses.shape, bf16),
            pltpu.VMEM(coupling.shape, bf16),
        ),
        [IN_VMEM, IN_VMEM, IN_HBM, IN_HBM, IN_HBM],
        [
            pltpu.VMEM((orbitals, LANES), jnp.int32),
            pltpu.VMEM((height, LANES), f32),
            pltpu.VMEM((energies, 2, height, LANES), f32),
            pltpu.SemaphoreType.DMA((3,)),
        ],
        flops=4 * cube,
    )(neighbors, phonon, in_hbm[2], in_hbm[0], in_hbm[1])
    samples = lax.all_gather(samples, "energy", axis=0, tiled=True)
    columns, samples = lax.optimization_barrier((columns, samples))

    greens, pairs = [], []
    for e in range(energies):
        if e:
            from_above[e], *pairs = lax.optimization_barrier((from_above[e], *pairs))
        right_self = call(unpack_kernel, shape((2, *plane), bf16), [IN_VMEM])(from_above[e])
        green, pair = call(
            functools.partial(green_kernel, e, width),
            (shape((2, *plane), bf16), shape((1 + e, 2, height, LANES), bf16)),
            [IN_VMEM] * (6 + e),
            [
                pltpu.VMEM((2, *plane), bf16),
                pltpu.VMEM((2, orbitals, padded), f32),
                pltpu.VMEM((2, height, LANES), f32),
            ],
            flops=12 * cube,
            limit=8,
        )(
            from_below[e],
            right_self,
            lead, inverses, coupling, columns, *pairs)
        greens.append(green)
        pairs.append(pair)
    sources = lax.all_gather(pairs[-1], "energy", axis=0, tiled=True)

    return call(
        final_kernel,
        shape((energies, 1, 2, *plane), bf16),
        [IN_SMEM] + [IN_VMEM] * 5,
        [
            pltpu.VMEM((shifts.shape[0], 2, height, LANES), f32),
            pltpu.VMEM((2, 2, used, LANES), f32),
            pltpu.VMEM((2, 2, orbitals, padded), bf16),
            pltpu.VMEM((2, 2, *plane), bf16),
            pltpu.SemaphoreType.DMA((2, 2)),
        ],
        flops=16 * cube,
        out_spec=IN_HBM,
        limit=16,
    )(shifts, samples, sources, slots, *greens)


def solution(mesh):
    return jax.shard_map(
        body,
        mesh=mesh,
        in_specs=(
            P("energy", "domain", None, None, None),
            P("domain", None, None),
            P("energy", None, None, None),
            P("energy", "domain", None, None),
            P("domain", None, None),
            P(),
        ),
        out_specs=P("energy", "domain", None, None, None),
        check_vma=False,
    )
```

```python
import functools

import jax
import jax.numpy as jnp
from jax import lax
from jax.experimental import pallas as pl
from jax.experimental.pallas import tpu as pltpu
from jax.sharding import PartitionSpec as P

LANES = 128
NEAR = (0, 2, 6)
SUBLANES = 8
MIB = 1024 * 1024


def product(first, second):
    return jnp.dot(first, second, preferred_element_type=jnp.float32)


def product_nt(first, second):
    return lax.dot_general(
        first, second, (((1,), (1,)), ((), ())), preferred_element_type=jnp.float32
    )


def product_tn(first, second):
    return lax.dot_general(
        first, second, (((0,), (0,)), ((), ())), preferred_element_type=jnp.float32
    )


def complex_product(first, second):
    reals = product(first[0], second[0])
    imags = product(first[1], second[1])
    both = product(first[0] + first[1], second[0] + second[1])
    return reals - imags, both - reals - imags


def packed_rows(orbitals):
    return 2 * orbitals * orbitals // LANES


def pack_planes(out_ref, planes):
    orbitals = planes[0].shape[0]
    whole = orbitals // LANES
    rest = orbitals - whole * LANES
    pieces = LANES // rest // 2
    height = orbitals // pieces
    for c, plane in enumerate(planes):
        for t in range(whole):
            out_ref[pl.ds((c * whole + t) * orbitals, orbitals), :] = plane[
                :, t * LANES : (t + 1) * LANES
            ]
    tails = [
        plane[h * height : (h + 1) * height, whole * LANES :]
        for plane in planes
        for h in range(pieces)
    ]
    out_ref[pl.ds(2 * whole * orbitals, height), :] = jnp.concatenate(tails, axis=1)


def unpack_planes(packed_ref, plane_ref):
    orbitals = plane_ref.shape[1]
    whole = orbitals // LANES
    rest = orbitals - whole * LANES
    pieces = LANES // rest // 2
    height = orbitals // pieces
    tails = packed_ref[pl.ds(2 * whole * orbitals, height), :]
    for c in range(2):
        for t in range(whole):
            plane_ref[c, :, t * LANES : (t + 1) * LANES] = packed_ref[
                pl.ds((c * whole + t) * orbitals, orbitals), :
            ]
        for h in range(pieces):
            start = (c * pieces + h) * rest
            plane_ref[c, h * height : (h + 1) * height, whole * LANES :] = tails[
                :, start : start + rest
            ]


def send_kernel(
    e, inverses_ref, coupling_ref, first_ref, second_ref, inverse, right_self, coupling, sems
):
    copies = [pltpu.make_async_copy(coupling_ref.at[0], coupling, sems.at[2])]
    for c in range(2):
        copies.append(pltpu.make_async_copy(inverses_ref.at[e, 0, c], inverse.at[c], sems.at[c]))
    for copy in copies:
        copy.start()
    copies[0].wait()
    for c in range(2):
        copies[1 + c].wait()
        right_product = product_nt(inverse[c], coupling[...]).astype(jnp.bfloat16)
        right_self[c] = product(coupling[...], right_product).astype(jnp.bfloat16)
    even = lax.axis_index("domain") % 2 == 0

    def pack(next_ref, before_ref):
        pack_planes(next_ref, [inverse[c] for c in range(2)])
        pack_planes(before_ref, [right_self[c] for c in range(2)])

    @pl.when(even)
    def _():
        pack(first_ref, second_ref)

    @pl.when(jnp.logical_not(even))
    def _():
        pack(second_ref, first_ref)


def group_iotas():
    sublane = lax.broadcasted_iota(jnp.int32, (SUBLANES, LANES), 0)
    lane = lax.broadcasted_iota(jnp.int32, (SUBLANES, LANES), 1)
    return sublane, lane


def along_lanes(values, lanes):
    return jnp.take_along_axis(values, lanes, axis=1, mode="promise_in_bounds")


def table_kernel(
    width, neighbors_ref, phonon_ref, lead_ref, coupling_ref,
    columns_ref, slots_ref, samples_ref, lead_held, coupling_held,
    wide, flat, samples, sems,
):
    fetches = [
        pltpu.make_async_copy(source, held, sems.at[i])
        for i, (source, held) in enumerate(
            ((coupling_ref, coupling_held), (lead_ref, lead_held))
        )
    ]
    for fetch in fetches:
        fetch.start()
    orbitals = neighbors_ref.shape[1]
    groups = orbitals // SUBLANES
    energies = phonon_ref.shape[0]
    sublane, lane = group_iotas()
    own = sublane == lane // width
    wide[...] = jnp.zeros(wide.shape, wide.dtype)
    wide[:, :width] = neighbors_ref[0]
    flat[...] = jnp.full(flat.shape, -1.0, flat.dtype)
    samples[...] = jnp.zeros(samples.shape, samples.dtype)
    tiles = slots_ref.shape[1] // LANES
    for r in range(groups):
        rows = slice(r * SUBLANES, (r + 1) * SUBLANES)
        group = wide[rows, :]
        columns = along_lanes(group, lane % width)
        columns_ref[rows, :] = columns
        flat[r : r + 1, :] = jnp.sum(
            jnp.where(own, columns.astype(jnp.float32), 0.0), axis=0, keepdims=True
        )
        found = [jnp.full((SUBLANES, LANES), -1, jnp.int32) for _ in range(tiles)]
        for k in range(width):
            column = jnp.broadcast_to(group[:, k : k + 1], (SUBLANES, LANES))
            slot = sublane * width + k
            for t in range(tiles):
                found[t] = jnp.where(column == lane + t * LANES, slot, found[t])
        for t in range(tiles):
            slots_ref[rows, t * LANES : (t + 1) * LANES] = found[t]
        for e in range(energies):
            samples[e, :, r, :] = phonon_ref[e, 0, :, r * LANES : (r + 1) * LANES].astype(
                jnp.float32
            )
    for r in range(flat.shape[0] // SUBLANES):
        rows = slice(r * SUBLANES, (r + 1) * SUBLANES)
        here = flat[rows, :]
        values = [[samples[e, c, rows, :] for c in range(2)] for e in range(energies)]
        totals = [list(pair) for pair in values]
        for d in range(1, width):
            turned = (lane // width) * width + (lane + d) % width
            same = here == along_lanes(here, turned)
            for e in range(energies):
                for c in range(2):
                    totals[e][c] = totals[e][c] + jnp.where(
                        same, along_lanes(values[e][c], turned), 0.0
                    )
        for e in range(energies):
            for c in range(2):
                samples[e, c, rows, :] = totals[e][c]
    samples_ref[...] = samples[...].astype(jnp.bfloat16)
    for fetch in fetches:
        fetch.wait()


def unpack_kernel(packed_ref, plane_ref):
    unpack_planes(packed_ref, plane_ref)


def green_kernel(
    e, width, second_ref, first_planes, lead_ref, inverses_ref, coupling_ref, columns_ref, *rest
):
    *pair_before, green_ref, pair_ref, previous, right_self, inverse, wide, flat, sems = rest
    orbitals = inverse.shape[1]
    copies = [
        pltpu.make_async_copy(inverses_ref.at[e, 0, c], inverse.at[c], sems.at[c]) for c in range(2)
    ]
    for copy in copies:
        copy.start()
    domain = lax.axis_index("domain")
    even = domain % 2 == 0

    @pl.when(domain == 0)
    def _():
        previous[...] = lead_ref[e]

    @pl.when(even & (domain > 0))
    def _():
        unpack_planes(second_ref, previous)

    @pl.when(even)
    def _():
        right_self[...] = first_planes[...]

    @pl.when(jnp.logical_not(even))
    def _():
        previous[...] = first_planes[...]
        unpack_planes(second_ref, right_self)

    coupling = coupling_ref[0]
    coupled = []
    for c in range(2):
        left_product = product(previous[c], coupling).astype(jnp.bfloat16)
        left_self = product_tn(coupling, left_product).astype(jnp.bfloat16)
        coupled.append(
            (left_self.astype(jnp.float32) + right_self[c].astype(jnp.float32)).astype(jnp.bfloat16)
        )
    for copy in copies:
        copy.wait()
    own = [inverse[c] for c in range(2)]
    inner = [part.astype(jnp.bfloat16) for part in complex_product(coupled, own)]
    for c, part in enumerate(complex_product(own, inner)):
        green = (own[c].astype(jnp.float32) + part).astype(jnp.bfloat16)
        green_ref[c] = green
        wide[c, :, :orbitals] = green.astype(jnp.float32)
    for k, ref in enumerate(pair_before):
        pair_ref[k] = ref[0]
    gather_pairs(width, wide, columns_ref, flat, pair_ref, len(pair_before))


def gather_pairs(width, wide, columns_ref, flat, pair_ref, place):
    orbitals = columns_ref.shape[0]
    tiles = wide.shape[2] // LANES
    sublane, lane = group_iotas()
    own = sublane == lane // width
    flat[...] = jnp.zeros(flat.shape, flat.dtype)
    for r in range(orbitals // SUBLANES):
        rows = slice(r * SUBLANES, (r + 1) * SUBLANES)
        columns = columns_ref[rows, :]
        within = columns & (LANES - 1)
        tile = columns // LANES
        for c in range(2):
            taken = jnp.zeros((SUBLANES, LANES), jnp.float32)
            for t in range(tiles):
                candidate = along_lanes(wide[c, rows, t * LANES : (t + 1) * LANES], within)
                taken = jnp.where(own & (tile == t), candidate, taken)
            flat[c, r : r + 1, :] = jnp.sum(taken, axis=0, keepdims=True)
    pair_ref[place] = flat[...].astype(jnp.bfloat16)


def final_kernel(shifts_ref, samples_ref, slots_ref, green_even_ref, green_odd_ref, *rest):
    *pairs, out_ref, sources, merged, self_block, result, sems = rest
    points = shifts_ref.shape[0]
    orbitals = result.shape[2]
    groups = orbitals // SUBLANES
    tiles = slots_ref.shape[1] // LANES
    used = merged.shape[2]
    me = lax.axis_index("energy")
    if len(pairs) == 1:

        def widen(p, carry):
            for c in range(2):
                sources[p, c] = pairs[0][p, c].astype(jnp.float32)
            return carry

        lax.fori_loop(0, points, widen, 0, unroll=4)
    else:
        for k, array in enumerate(pairs):
            owner = (me ^ NEAR[k // 2 % 3]) ^ (k % 2)
            for e in range(2):
                for c in range(2):
                    sources[2 * owner + e, c] = array[e, c].astype(jnp.float32)

    def add_point(w, sums):
        shift = shifts_ref[w]
        sample = [samples_ref[w, c].astype(jnp.float32)[:used] for c in range(2)]
        after = []
        for e in range(2):
            source = 2 * me + e - shift
            keep = jnp.where((source >= 0) & (source < points), 1.0, 0.0)
            source = jnp.clip(source, 0, points - 1)
            real, imag = (sources[source, c, :used, :] for c in range(2))
            after.append(
                (
                    sums[e][0] + keep * (sample[0] * real - sample[1] * imag),
                    sums[e][1] + keep * (sample[0] * imag + sample[1] * real),
                )
            )
        return tuple(after)

    zero = jnp.zeros((used, LANES), jnp.float32)
    sums = lax.fori_loop(0, points, add_point, ((zero, zero), (zero, zero)), unroll=4)
    for e in range(2):
        for c in range(2):
            merged[e, c] = sums[e][c]
    copies = []
    for e, green_ref in enumerate((green_even_ref, green_odd_ref)):
        for q in range(groups // 2):
            for t in range(tiles):
                found = [[], []]
                for r in (2 * q, 2 * q + 1):
                    slot = slots_ref[r * SUBLANES : (r + 1) * SUBLANES, t * LANES : (t + 1) * LANES]
                    within = slot & (LANES - 1)
                    for c in range(2):
                        row = jnp.broadcast_to(merged[e, c, r : r + 1, :], (SUBLANES, LANES))
                        found[c].append(jnp.where(slot >= 0, along_lanes(row, within), 0.0))
                for c in range(2):
                    self_block[e, c, q * 16 : (q + 1) * 16, t * LANES : (t + 1) * LANES] = (
                        jnp.concatenate(found[c], axis=0).astype(jnp.bfloat16)
                    )
    for e, green_ref in enumerate((green_even_ref, green_odd_ref)):
        green = [green_ref[c] for c in range(2)]
        sigma = [self_block[e, c, :, :orbitals] for c in range(2)]
        scattered = [part.astype(jnp.bfloat16) for part in complex_product(green, sigma)]
        for c, part in enumerate(complex_product(scattered, green)):
            result[e, c] = (green[c].astype(jnp.float32) + part).astype(jnp.bfloat16)
            copies.append(pltpu.make_async_copy(result.at[e, c], out_ref.at[e, 0, c], sems.at[e, c]))
            copies[-1].start()
    for copy in copies:
        copy.wait()


IN_VMEM = pl.BlockSpec(memory_space=pltpu.VMEM)
IN_SMEM = pl.BlockSpec(memory_space=pltpu.SMEM)
IN_HBM = pl.BlockSpec(memory_space=pltpu.HBM)


def call(kernel, out_shape, in_specs, scratch=(), flops=0, bytes_accessed=1 << 20, out_spec=None, limit=4):
    return pl.pallas_call(
        kernel,
        out_shape=out_shape,
        in_specs=in_specs,
        out_specs=out_spec or (IN_VMEM if not isinstance(out_shape, tuple) else (IN_VMEM,) * len(out_shape)),
        scratch_shapes=list(scratch),
        compiler_params=pltpu.CompilerParams(vmem_limit_bytes=limit * MIB),
        cost_estimate=pl.CostEstimate(flops=flops, bytes_accessed=bytes_accessed, transcendentals=0),
    )


def body(inverses, coupling, lead_green, phonon, neighbors, shifts):
    energies = inverses.shape[0]
    orbitals = inverses.shape[3]
    width = neighbors.shape[2]
    rows = packed_rows(orbitals)
    groups = orbitals * width // LANES
    used = -(-groups // SUBLANES) * SUBLANES
    height = -(-groups // 16) * 16
    padded = -(-orbitals // LANES) * LANES
    bf16, f32 = jnp.bfloat16, jnp.float32
    shape = jax.ShapeDtypeStruct
    cube = 2 * orbitals**3
    plane = (orbitals, orbitals)
    domains = lax.axis_size("domain")
    routes = [
        [swap for i in range(start, domains - 1, 2) for swap in ((i, i + 1), (i + 1, i))]
        for start in range(2)
    ]

    in_hbm = [
        pltpu.with_memory_space_constraint(array, pltpu.HBM)
        for array in (inverses, coupling, lead_green)
    ]

    barred = in_hbm[0]
    received = []
    for e in range(energies):
        sent = call(
            functools.partial(send_kernel, e),
            (shape((rows, LANES), bf16), shape((rows, LANES), bf16)),
            [IN_HBM] * 2,
            [
                pltpu.VMEM((2, *plane), bf16),
                pltpu.VMEM((2, *plane), bf16),
                pltpu.VMEM(plane, bf16),
                pltpu.SemaphoreType.DMA((3,)),
            ],
            flops=4 * cube,
        )(barred, in_hbm[1])
        received.append([lax.ppermute(x, "domain", route) for x, route in zip(sent, routes)])
        barred, neighbors, _ = lax.optimization_barrier((barred, neighbors, sent[0]))
        barred = pltpu.with_memory_space_constraint(barred, pltpu.HBM)
    columns, slots, samples, lead, coupling = call(
        functools.partial(table_kernel, width),
        (
            shape((orbitals, LANES), jnp.int32),
            shape((orbitals, padded), jnp.int32),
            shape((energies, 2, height, LANES), bf16),
            pltpu.VMEM(lead_green.shape, bf16),
            pltpu.VMEM(coupling.shape, bf16),
        ),
        [IN_VMEM, IN_VMEM, IN_HBM, IN_HBM],
        [
            pltpu.VMEM((orbitals, LANES), jnp.int32),
            pltpu.VMEM((height, LANES), f32),
            pltpu.VMEM((energies, 2, height, LANES), f32),
            pltpu.SemaphoreType.DMA((2,)),
        ],
        flops=4 * cube,
    )(neighbors, phonon, in_hbm[2], in_hbm[1])
    samples = lax.all_gather(samples, "energy", axis=0, tiled=True)
    columns, samples = lax.optimization_barrier((columns, samples))

    greens, pairs = [], []
    for e in range(energies):
        first, second = received[e]
        if e:
            first, *pairs = lax.optimization_barrier((first, *pairs))
        first = call(unpack_kernel, shape((2, *plane), bf16), [IN_VMEM])(first)
        green, pair = call(
            functools.partial(green_kernel, e, width),
            (shape((2, *plane), bf16), shape((1 + e, 2, height, LANES), bf16)),
            [IN_VMEM] * 3 + [IN_HBM] + [IN_VMEM] * (2 + e),
            [
                pltpu.VMEM((2, *plane), bf16),
                pltpu.VMEM((2, *plane), bf16),
                pltpu.VMEM((2, *plane), bf16),
                pltpu.VMEM((2, orbitals, padded), f32),
                pltpu.VMEM((2, height, LANES), f32),
                pltpu.SemaphoreType.DMA((2,)),
            ],
            flops=12 * cube,
            limit=12,
        )(second, first, lead, in_hbm[0], coupling, columns, *pairs)
        greens.append(green)
        pairs.append(pair)
    pair = pairs[-1]
    devices = lax.axis_size("energy")
    if devices == 8 and energies == 2:
        across = lax.ppermute(pair, "energy", [(i, i ^ 6) for i in range(2, 6)])
        beside = lax.ppermute(pair, "energy", [(i, i ^ 2) for i in range(8)])
        sources = []
        for array in (pair, beside, across):
            sources += [array, lax.ppermute(array, "energy", [(i, i ^ 1) for i in range(8)])]
    else:
        sources = [lax.all_gather(pair, "energy", axis=0, tiled=True)]

    return call(
        final_kernel,
        shape((energies, 1, 2, *plane), bf16),
        [IN_SMEM] + [IN_VMEM] * (4 + len(sources)),
        [
            pltpu.VMEM((shifts.shape[0], 2, height, LANES), f32),
            pltpu.VMEM((2, 2, used, LANES), f32),
            pltpu.VMEM((2, 2, orbitals, padded), bf16),
            pltpu.VMEM((2, 2, *plane), bf16),
            pltpu.SemaphoreType.DMA((2, 2)),
        ],
        flops=16 * cube,
        out_spec=IN_HBM,
        limit=16,
    )(shifts, samples, slots, *greens, *sources)


def solution(mesh):
    return jax.shard_map(
        body,
        mesh=mesh,
        in_specs=(
            P("energy", "domain", None, None, None),
            P("domain", None, None),
            P("energy", None, None, None),
            P("energy", "domain", None, None),
            P("domain", None, None),
            P(),
        ),
        out_specs=P("energy", "domain", None, None, None),
        check_vma=False,
    )
```

```python
import functools

import jax
import jax.numpy as jnp
from jax import lax
from jax.experimental import pallas as pl
from jax.experimental.pallas import tpu as pltpu
from jax.sharding import PartitionSpec as P

LANES = 128
NEAR = (0, 2, 6)
SUBLANES = 8
MIB = 1024 * 1024


def product(first, second):
    return jnp.dot(first, second, preferred_element_type=jnp.float32)


def product_nt(first, second):
    return lax.dot_general(
        first, second, (((1,), (1,)), ((), ())), preferred_element_type=jnp.float32
    )


def product_tn(first, second):
    return lax.dot_general(
        first, second, (((0,), (0,)), ((), ())), preferred_element_type=jnp.float32
    )


def complex_product(first, second):
    reals = product(first[0], second[0])
    imags = product(first[1], second[1])
    both = product(first[0] + first[1], second[0] + second[1])
    return reals - imags, both - reals - imags


def packed_rows(orbitals):
    return 2 * orbitals * orbitals // LANES


def pack_planes(out_ref, planes, place):
    orbitals = planes[0].shape[0]
    whole = orbitals // LANES
    for c, plane in enumerate(planes, place):
        for t in range(whole):
            out_ref[pl.ds((c * whole + t) * orbitals, orbitals), :] = plane[
                :, t * LANES : (t + 1) * LANES
            ]


def pack_tails(out_ref, planes):
    orbitals = planes[0].shape[0]
    whole = orbitals // LANES
    rest = orbitals - whole * LANES
    pieces = LANES // rest // 2
    height = orbitals // pieces
    tails = [
        plane[h * height : (h + 1) * height, whole * LANES :]
        for plane in planes
        for h in range(pieces)
    ]
    out_ref[pl.ds(2 * whole * orbitals, height), :] = jnp.concatenate(tails, axis=1)


def unpack_planes(packed_ref, plane_ref):
    orbitals = plane_ref.shape[1]
    whole = orbitals // LANES
    rest = orbitals - whole * LANES
    pieces = LANES // rest // 2
    height = orbitals // pieces
    tails = packed_ref[pl.ds(2 * whole * orbitals, height), :]
    for c in range(2):
        for t in range(whole):
            plane_ref[c, :, t * LANES : (t + 1) * LANES] = packed_ref[
                pl.ds((c * whole + t) * orbitals, orbitals), :
            ]
        for h in range(pieces):
            start = (c * pieces + h) * rest
            plane_ref[c, h * height : (h + 1) * height, whole * LANES :] = tails[
                :, start : start + rest
            ]


def send_kernel(
    e, inverses_ref, coupling_ref, first_ref, second_ref,
    inverse, coupling, up, down, sems, up_sem, down_sems,
):
    copies = [pltpu.make_async_copy(coupling_ref.at[0], coupling, sems.at[2])]
    for c in range(2):
        copies.append(pltpu.make_async_copy(inverses_ref.at[e, 0, c], inverse.at[c], sems.at[c]))
    for copy in copies:
        copy.start()
    even = lax.axis_index("domain") % 2 == 0
    split = inverse.shape[1] * (inverse.shape[2] // LANES)

    def on_parity(act):
        for parity, next_ref, before_ref in ((True, first_ref, second_ref), (False, second_ref, first_ref)):

            @pl.when(even == parity)
            def _():
                act(
                    pltpu.make_async_copy(up, next_ref, up_sem),
                    pltpu.make_async_copy(
                        down.at[pl.ds(0, split)], before_ref.at[pl.ds(0, split)], down_sems.at[0]
                    ),
                    pltpu.make_async_copy(
                        down.at[pl.ds(split, down.shape[0] - split)],
                        before_ref.at[pl.ds(split, down.shape[0] - split)],
                        down_sems.at[1],
                    ),
                )

    def right_self(c):
        right_product = product_nt(inverse[c], coupling[...]).astype(jnp.bfloat16)
        return product(coupling[...], right_product).astype(jnp.bfloat16)

    copies[0].wait()
    copies[1].wait()
    real = right_self(0)
    pack_planes(down, [real], 0)
    copies[2].wait()
    pack_planes(up, [inverse[0], inverse[1]], 0)
    pack_tails(up, [inverse[0], inverse[1]])
    on_parity(lambda whole, head, tail: (whole.start(), head.start()))
    imag = right_self(1)
    pack_planes(down, [imag], 1)
    pack_tails(down, [real, imag])
    on_parity(lambda whole, head, tail: tail.start())
    on_parity(lambda whole, head, tail: (whole.wait(), head.wait(), tail.wait()))


def group_iotas():
    sublane = lax.broadcasted_iota(jnp.int32, (SUBLANES, LANES), 0)
    lane = lax.broadcasted_iota(jnp.int32, (SUBLANES, LANES), 1)
    return sublane, lane


def along_lanes(values, lanes):
    return jnp.take_along_axis(values, lanes, axis=1, mode="promise_in_bounds")


def table_kernel(
    width, neighbors_ref, phonon_ref, lead_ref, coupling_ref,
    columns_ref, slots_ref, samples_ref, lead_held, coupling_held,
    wide, flat, samples, sems,
):
    fetches = [
        pltpu.make_async_copy(source, held, sems.at[i])
        for i, (source, held) in enumerate(
            ((coupling_ref, coupling_held), (lead_ref, lead_held))
        )
    ]
    for fetch in fetches:
        fetch.start()
    orbitals = neighbors_ref.shape[1]
    groups = orbitals // SUBLANES
    energies = phonon_ref.shape[0]
    sublane, lane = group_iotas()
    own = sublane == lane // width
    wide[...] = jnp.zeros(wide.shape, wide.dtype)
    wide[:, :width] = neighbors_ref[0]
    flat[...] = jnp.full(flat.shape, -1.0, flat.dtype)
    samples[...] = jnp.zeros(samples.shape, samples.dtype)
    tiles = slots_ref.shape[1] // LANES
    for r in range(groups):
        rows = slice(r * SUBLANES, (r + 1) * SUBLANES)
        group = wide[rows, :]
        columns = along_lanes(group, lane % width)
        columns_ref[rows, :] = columns
        flat[r : r + 1, :] = jnp.sum(
            jnp.where(own, columns.astype(jnp.float32), 0.0), axis=0, keepdims=True
        )
        found = [jnp.full((SUBLANES, LANES), -1, jnp.int32) for _ in range(tiles)]
        for k in range(width):
            column = jnp.broadcast_to(group[:, k : k + 1], (SUBLANES, LANES))
            slot = sublane * width + k
            for t in range(tiles):
                found[t] = jnp.where(column == lane + t * LANES, slot, found[t])
        for t in range(tiles):
            slots_ref[rows, t * LANES : (t + 1) * LANES] = found[t]
        for e in range(energies):
            samples[e, :, r, :] = phonon_ref[e, 0, :, r * LANES : (r + 1) * LANES].astype(
                jnp.float32
            )
    for r in range(flat.shape[0] // SUBLANES):
        rows = slice(r * SUBLANES, (r + 1) * SUBLANES)
        here = flat[rows, :]
        values = [[samples[e, c, rows, :] for c in range(2)] for e in range(energies)]
        totals = [list(pair) for pair in values]
        for d in range(1, width):
            turned = (lane // width) * width + (lane + d) % width
            same = here == along_lanes(here, turned)
            for e in range(energies):
                for c in range(2):
                    totals[e][c] = totals[e][c] + jnp.where(
                        same, along_lanes(values[e][c], turned), 0.0
                    )
        for e in range(energies):
            for c in range(2):
                samples[e, c, rows, :] = totals[e][c]
    samples_ref[...] = samples[...].astype(jnp.bfloat16)
    for fetch in fetches:
        fetch.wait()


def unpack_kernel(packed_ref, plane_ref):
    unpack_planes(packed_ref, plane_ref)


def green_kernel(
    width, second_ref, first_planes, lead_ref, inverses_ref, coupling_ref, columns_ref,
    green_ref, pair_ref, previous, right_self, inverse, wide, flat, sems,
):
    orbitals = inverse.shape[1]
    copies = [
        pltpu.make_async_copy(inverses_ref.at[0, 0, c], inverse.at[c], sems.at[c]) for c in range(2)
    ]
    for copy in copies:
        copy.start()
    domain = lax.axis_index("domain")
    even = domain % 2 == 0

    @pl.when(domain == 0)
    def _():
        previous[...] = lead_ref[0]

    @pl.when(even & (domain > 0))
    def _():
        unpack_planes(second_ref, previous)

    @pl.when(even)
    def _():
        right_self[...] = first_planes[...]

    @pl.when(jnp.logical_not(even))
    def _():
        previous[...] = first_planes[...]
        unpack_planes(second_ref, right_self)

    coupling = coupling_ref[0]
    coupled = []
    for c in range(2):
        left_product = product(previous[c], coupling).astype(jnp.bfloat16)
        left_self = product_tn(coupling, left_product).astype(jnp.bfloat16)
        coupled.append(
            (left_self.astype(jnp.float32) + right_self[c].astype(jnp.float32)).astype(jnp.bfloat16)
        )
    for copy in copies:
        copy.wait()
    own = [inverse[c] for c in range(2)]
    inner = [part.astype(jnp.bfloat16) for part in complex_product(coupled, own)]
    for c, part in enumerate(complex_product(own, inner)):
        green = (own[c].astype(jnp.float32) + part).astype(jnp.bfloat16)
        green_ref[c] = green
        wide[c, :, :orbitals] = green.astype(jnp.float32)
    gather_pairs(width, wide, columns_ref, flat, pair_ref, 0)


def sides_kernel(inverses_ref, coupling_ref, before_ref, after_ref, inverse_ref, sems):
    last = inverses_ref.shape[0] - 1
    copies = [
        pltpu.make_async_copy(inverses_ref.at[last, 0, c], inverse_ref.at[c], sems.at[c])
        for c in range(2)
    ]
    for copy in copies:
        copy.start()
    coupling = coupling_ref[0]
    for c in range(2):
        copies[c].wait()
        before_ref[c] = product_nt(inverse_ref[c], coupling).astype(jnp.bfloat16)
        after_ref[c] = product(coupling, inverse_ref[c]).astype(jnp.bfloat16)


def add_side(left, value, middle, right):
    inner = complex_product([middle[c] for c in range(2)], [right[c] for c in range(2)])
    outer = complex_product(
        [left[c] for c in range(2)], [part.astype(jnp.bfloat16) for part in inner]
    )
    return [value[c].astype(jnp.float32) + outer[c] for c in range(2)]


def early_kernel(
    first_planes, lead_ref, before_ref, after_ref, inverse_ref, sum_ref
):
    domain = lax.axis_index("domain")
    none = (domain % 2 == 1) & (domain == lax.axis_size("domain") - 1)

    def write(values):
        for c in range(2):
            sum_ref[c] = values[c]

    @pl.when(domain == 0)
    def _():
        lead = lead_ref[lead_ref.shape[0] - 1]
        write(add_side(before_ref, inverse_ref, lead, after_ref))

    @pl.when((domain % 2 == 1) & jnp.logical_not(none))
    def _():
        write(add_side(before_ref, inverse_ref, first_planes, after_ref))

    @pl.when((domain % 2 == 0) & (domain > 0))
    def _():
        write(add_side(inverse_ref, inverse_ref, first_planes, inverse_ref))

    @pl.when(none)
    def _():
        write([inverse_ref[c].astype(jnp.float32) for c in range(2)])


def late_kernel(
    width, second_ref, first_planes, before_ref, after_ref, inverse_ref, sum_ref, columns_ref, pair_before,
    green_ref, pair_ref, middle, wide, flat,
):
    orbitals = inverse_ref.shape[1]
    domain = lax.axis_index("domain")
    ends = (domain == 0) | ((domain % 2 == 1) & (domain == lax.axis_size("domain") - 1))

    @pl.when(ends)
    def _():
        middle[...] = first_planes[...]

    @pl.when(jnp.logical_not(ends))
    def _():
        unpack_planes(second_ref, middle)

    from_before = (domain > 0) & ((domain % 2 == 0) | ends)

    def write(values):
        for c in range(2):
            green = values[c].astype(jnp.bfloat16)
            green_ref[c] = green
            wide[c, :, :orbitals] = green.astype(jnp.float32)

    @pl.when(from_before)
    def _():
        write(add_side(before_ref, sum_ref, middle, after_ref))

    @pl.when(jnp.logical_not(from_before))
    def _():
        write(add_side(inverse_ref, sum_ref, middle, inverse_ref))

    pair_ref[0] = pair_before[0]
    gather_pairs(width, wide, columns_ref, flat, pair_ref, 1)


def gather_pairs(width, wide, columns_ref, flat, pair_ref, place):
    orbitals = columns_ref.shape[0]
    tiles = wide.shape[2] // LANES
    sublane, lane = group_iotas()
    own = sublane == lane // width
    flat[...] = jnp.zeros(flat.shape, flat.dtype)
    for r in range(orbitals // SUBLANES):
        rows = slice(r * SUBLANES, (r + 1) * SUBLANES)
        columns = columns_ref[rows, :]
        within = columns & (LANES - 1)
        tile = columns // LANES
        for c in range(2):
            taken = jnp.zeros((SUBLANES, LANES), jnp.float32)
            for t in range(tiles):
                candidate = along_lanes(wide[c, rows, t * LANES : (t + 1) * LANES], within)
                taken = jnp.where(own & (tile == t), candidate, taken)
            flat[c, r : r + 1, :] = jnp.sum(taken, axis=0, keepdims=True)
    pair_ref[place] = flat[...].astype(jnp.bfloat16)


def final_kernel(shifts_ref, samples_ref, slots_ref, green_even_ref, green_odd_ref, *rest):
    *pairs, out_ref, sources, merged, self_block, result, sems = rest
    points = shifts_ref.shape[0]
    orbitals = result.shape[2]
    groups = orbitals // SUBLANES
    tiles = slots_ref.shape[1] // LANES
    used = merged.shape[2]
    me = lax.axis_index("energy")
    if len(pairs) == 1:

        def widen(p, carry):
            for c in range(2):
                sources[p, c] = pairs[0][p, c].astype(jnp.float32)
            return carry

        lax.fori_loop(0, points, widen, 0, unroll=4)
    else:
        for k, array in enumerate(pairs):
            owner = (me ^ NEAR[k // 2 % 3]) ^ (k % 2)
            for e in range(2):
                for c in range(2):
                    sources[2 * owner + e, c] = array[e, c].astype(jnp.float32)

    def add_point(w, sums):
        shift = shifts_ref[w]
        sample = [samples_ref[w, c].astype(jnp.float32)[:used] for c in range(2)]
        after = []
        for e in range(2):
            source = 2 * me + e - shift
            keep = jnp.where((source >= 0) & (source < points), 1.0, 0.0)
            source = jnp.clip(source, 0, points - 1)
            real, imag = (sources[source, c, :used, :] for c in range(2))
            after.append(
                (
                    sums[e][0] + keep * (sample[0] * real - sample[1] * imag),
                    sums[e][1] + keep * (sample[0] * imag + sample[1] * real),
                )
            )
        return tuple(after)

    zero = jnp.zeros((used, LANES), jnp.float32)
    sums = lax.fori_loop(0, points, add_point, ((zero, zero), (zero, zero)), unroll=4)
    for e in range(2):
        for c in range(2):
            merged[e, c] = sums[e][c]
    copies = []
    for e, green_ref in enumerate((green_even_ref, green_odd_ref)):
        for q in range(groups // 2):
            for t in range(tiles):
                found = [[], []]
                for r in (2 * q, 2 * q + 1):
                    slot = slots_ref[r * SUBLANES : (r + 1) * SUBLANES, t * LANES : (t + 1) * LANES]
                    within = slot & (LANES - 1)
                    for c in range(2):
                        row = jnp.broadcast_to(merged[e, c, r : r + 1, :], (SUBLANES, LANES))
                        found[c].append(jnp.where(slot >= 0, along_lanes(row, within), 0.0))
                for c in range(2):
                    self_block[e, c, q * 16 : (q + 1) * 16, t * LANES : (t + 1) * LANES] = (
                        jnp.concatenate(found[c], axis=0).astype(jnp.bfloat16)
                    )
    for e, green_ref in enumerate((green_even_ref, green_odd_ref)):
        green = [green_ref[c] for c in range(2)]
        sigma = [self_block[e, c, :, :orbitals] for c in range(2)]
        scattered = [part.astype(jnp.bfloat16) for part in complex_product(green, sigma)]
        for c, part in enumerate(complex_product(scattered, green)):
            result[e, c] = (green[c].astype(jnp.float32) + part).astype(jnp.bfloat16)
            copies.append(pltpu.make_async_copy(result.at[e, c], out_ref.at[e, 0, c], sems.at[e, c]))
            copies[-1].start()
    for copy in copies:
        copy.wait()


IN_VMEM = pl.BlockSpec(memory_space=pltpu.VMEM)
IN_SMEM = pl.BlockSpec(memory_space=pltpu.SMEM)
IN_HBM = pl.BlockSpec(memory_space=pltpu.HBM)


def call(kernel, out_shape, in_specs, scratch=(), flops=0, bytes_accessed=1 << 20, out_spec=None, limit=4):
    return pl.pallas_call(
        kernel,
        out_shape=out_shape,
        in_specs=in_specs,
        out_specs=out_spec or (IN_VMEM if not isinstance(out_shape, tuple) else (IN_VMEM,) * len(out_shape)),
        scratch_shapes=list(scratch),
        compiler_params=pltpu.CompilerParams(vmem_limit_bytes=limit * MIB),
        cost_estimate=pl.CostEstimate(flops=flops, bytes_accessed=bytes_accessed, transcendentals=0),
    )


def body(inverses, coupling, lead_green, phonon, neighbors, shifts):
    energies = inverses.shape[0]
    orbitals = inverses.shape[3]
    width = neighbors.shape[2]
    rows = packed_rows(orbitals)
    groups = orbitals * width // LANES
    used = -(-groups // SUBLANES) * SUBLANES
    height = -(-groups // 16) * 16
    padded = -(-orbitals // LANES) * LANES
    bf16, f32 = jnp.bfloat16, jnp.float32
    shape = jax.ShapeDtypeStruct
    cube = 2 * orbitals**3
    plane = (orbitals, orbitals)
    domains = lax.axis_size("domain")
    routes = [
        [swap for i in range(start, domains - 1, 2) for swap in ((i, i + 1), (i + 1, i))]
        for start in range(2)
    ]

    in_hbm = [
        pltpu.with_memory_space_constraint(array, pltpu.HBM)
        for array in (inverses, coupling, lead_green)
    ]

    barred = in_hbm[0]
    received = []
    for e in range(energies):
        sent = call(
            functools.partial(send_kernel, e),
            (shape((rows, LANES), bf16), shape((rows, LANES), bf16)),
            [IN_HBM] * 2,
            [
                pltpu.VMEM((2, *plane), bf16),
                pltpu.VMEM(plane, bf16),
                pltpu.VMEM((rows, LANES), bf16),
                pltpu.VMEM((rows, LANES), bf16),
                pltpu.SemaphoreType.DMA((3,)),
                pltpu.SemaphoreType.DMA,
                pltpu.SemaphoreType.DMA((2,)),
            ],
            flops=4 * cube,
            out_spec=(IN_HBM,) * 2,
        )(barred, in_hbm[1])
        received.append([lax.ppermute(x, "domain", route) for x, route in zip(sent, routes)])
        barred, neighbors, _ = lax.optimization_barrier((barred, neighbors, sent[0]))
        barred = pltpu.with_memory_space_constraint(barred, pltpu.HBM)
    columns, slots, samples, lead, coupling = call(
        functools.partial(table_kernel, width),
        (
            shape((orbitals, LANES), jnp.int32),
            shape((orbitals, padded), jnp.int32),
            shape((energies, 2, height, LANES), bf16),
            pltpu.VMEM(lead_green.shape, bf16),
            pltpu.VMEM(coupling.shape, bf16),
        ),
        [IN_VMEM, IN_VMEM, IN_HBM, IN_HBM],
        [
            pltpu.VMEM((orbitals, LANES), jnp.int32),
            pltpu.VMEM((height, LANES), f32),
            pltpu.VMEM((energies, 2, height, LANES), f32),
            pltpu.SemaphoreType.DMA((2,)),
        ],
        flops=4 * cube,
    )(neighbors, phonon, in_hbm[2], in_hbm[1])
    samples = lax.all_gather(samples, "energy", axis=0, tiled=True)
    columns, samples = lax.optimization_barrier((columns, samples))

    pair_shape = (1, 2, height, LANES)
    block = shape((2, *plane), bf16)
    before, after, inverse = call(
        sides_kernel,
        (block,) * 3,
        [IN_HBM, IN_VMEM],
        [pltpu.SemaphoreType.DMA((2,))],
        flops=4 * cube,
    )(in_hbm[0], coupling)

    def unpacked(first):
        return call(unpack_kernel, block, [IN_VMEM])(first)

    first, second = received[0]
    green_even, pair = call(
        functools.partial(green_kernel, width),
        (block, shape(pair_shape, bf16)),
        [IN_VMEM] * 3 + [IN_HBM] + [IN_VMEM] * 2,
        [
            pltpu.VMEM((2, *plane), bf16),
            pltpu.VMEM((2, *plane), bf16),
            pltpu.VMEM((2, *plane), bf16),
            pltpu.VMEM((2, orbitals, padded), f32),
            pltpu.VMEM((2, height, LANES), f32),
            pltpu.SemaphoreType.DMA((2,)),
        ],
        flops=12 * cube,
        limit=12,
    )(second, unpacked(first), lead, in_hbm[0], coupling, columns)

    first, second = received[1]
    first, pair = lax.optimization_barrier((first, pair))
    first = unpacked(first)
    partial_sum = call(
        early_kernel, shape((2, *plane), f32), [IN_VMEM] * 5, flops=6 * cube, limit=12
    )(first, lead, before, after, inverse)
    green_odd, pair = call(
        functools.partial(late_kernel, width),
        (block, shape((2, *pair_shape[1:]), bf16)),
        [IN_VMEM] * 8,
        [
            pltpu.VMEM((2, *plane), bf16),
            pltpu.VMEM((2, orbitals, padded), f32),
            pltpu.VMEM((2, height, LANES), f32),
        ],
        flops=6 * cube,
        limit=12,
    )(second, first, before, after, inverse, partial_sum, columns, pair)
    devices = lax.axis_size("energy")
    if devices == 8 and energies == 2:
        across = lax.ppermute(pair, "energy", [(i, i ^ 6) for i in range(2, 6)])
        beside = lax.ppermute(pair, "energy", [(i, i ^ 2) for i in range(8)])
        sources = []
        for array in (pair, beside, across):
            sources += [array, lax.ppermute(array, "energy", [(i, i ^ 1) for i in range(8)])]
    else:
        sources = [lax.all_gather(pair, "energy", axis=0, tiled=True)]

    return call(
        final_kernel,
        shape((energies, 1, 2, *plane), bf16),
        [IN_SMEM] + [IN_VMEM] * (4 + len(sources)),
        [
            pltpu.VMEM((shifts.shape[0], 2, height, LANES), f32),
            pltpu.VMEM((2, 2, used, LANES), f32),
            pltpu.VMEM((2, 2, orbitals, padded), bf16),
            pltpu.VMEM((2, 2, *plane), bf16),
            pltpu.SemaphoreType.DMA((2, 2)),
        ],
        flops=16 * cube,
        out_spec=IN_HBM,
        limit=16,
    )(shifts, samples, slots, green_even, green_odd, *sources)


def solution(mesh):
    return jax.shard_map(
        body,
        mesh=mesh,
        in_specs=(
            P("energy", "domain", None, None, None),
            P("domain", None, None),
            P("energy", None, None, None),
            P("energy", "domain", None, None),
            P("domain", None, None),
            P(),
        ),
        out_specs=P("energy", "domain", None, None, None),
        check_vma=False,
    )
```

```python
import functools

import jax
import jax.numpy as jnp
from jax import lax
from jax.experimental import pallas as pl
from jax.experimental.pallas import tpu as pltpu
from jax.sharding import PartitionSpec as P

LANES = 128
NEAR = (0, 2, 6)
SUBLANES = 8
MIB = 1024 * 1024


def product(first, second):
    return jnp.dot(first, second, preferred_element_type=jnp.float32)


def product_nt(first, second):
    return lax.dot_general(
        first, second, (((1,), (1,)), ((), ())), preferred_element_type=jnp.float32
    )


def product_tn(first, second):
    return lax.dot_general(
        first, second, (((0,), (0,)), ((), ())), preferred_element_type=jnp.float32
    )


def complex_product(first, second):
    reals = product(first[0], second[0])
    imags = product(first[1], second[1])
    both = product(first[0] + first[1], second[0] + second[1])
    return reals - imags, both - reals - imags


def packed_rows(orbitals):
    return 2 * orbitals * orbitals // LANES


def pack_planes(out_ref, planes, place):
    orbitals = planes[0].shape[0]
    whole = orbitals // LANES
    for c, plane in enumerate(planes, place):
        for t in range(whole):
            out_ref[pl.ds((c * whole + t) * orbitals, orbitals), :] = plane[
                :, t * LANES : (t + 1) * LANES
            ]


def pack_tails(out_ref, planes):
    orbitals = planes[0].shape[0]
    whole = orbitals // LANES
    rest = orbitals - whole * LANES
    pieces = LANES // rest // 2
    height = orbitals // pieces
    tails = [
        plane[h * height : (h + 1) * height, whole * LANES :]
        for plane in planes
        for h in range(pieces)
    ]
    out_ref[pl.ds(2 * whole * orbitals, height), :] = jnp.concatenate(tails, axis=1)


def unpack_planes(packed_ref, plane_ref):
    orbitals = plane_ref.shape[1]
    whole = orbitals // LANES
    rest = orbitals - whole * LANES
    pieces = LANES // rest // 2
    height = orbitals // pieces
    tails = packed_ref[pl.ds(2 * whole * orbitals, height), :]
    for c in range(2):
        for t in range(whole):
            plane_ref[c, :, t * LANES : (t + 1) * LANES] = packed_ref[
                pl.ds((c * whole + t) * orbitals, orbitals), :
            ]
        for h in range(pieces):
            start = (c * pieces + h) * rest
            plane_ref[c, h * height : (h + 1) * height, whole * LANES :] = tails[
                :, start : start + rest
            ]


def send_kernel(
    e, inverses_ref, coupling_ref, first_ref, second_ref,
    inverse, coupling, up, down, sems, up_sem, down_sems,
):
    copies = [pltpu.make_async_copy(coupling_ref.at[0], coupling, sems.at[2])]
    for c in range(2):
        copies.append(pltpu.make_async_copy(inverses_ref.at[e, 0, c], inverse.at[c], sems.at[c]))
    for copy in copies:
        copy.start()
    even = lax.axis_index("domain") % 2 == 0
    split = inverse.shape[1] * (inverse.shape[2] // LANES)

    def on_parity(act):
        for parity, next_ref, before_ref in ((True, first_ref, second_ref), (False, second_ref, first_ref)):

            @pl.when(even == parity)
            def _():
                act(
                    pltpu.make_async_copy(up, next_ref, up_sem),
                    pltpu.make_async_copy(
                        down.at[pl.ds(0, split)], before_ref.at[pl.ds(0, split)], down_sems.at[0]
                    ),
                    pltpu.make_async_copy(
                        down.at[pl.ds(split, down.shape[0] - split)],
                        before_ref.at[pl.ds(split, down.shape[0] - split)],
                        down_sems.at[1],
                    ),
                )

    def right_self(c):
        right_product = product_nt(inverse[c], coupling[...]).astype(jnp.bfloat16)
        return product(coupling[...], right_product).astype(jnp.bfloat16)

    copies[0].wait()
    copies[1].wait()
    real = right_self(0)
    pack_planes(down, [real], 0)
    copies[2].wait()
    pack_planes(up, [inverse[0], inverse[1]], 0)
    pack_tails(up, [inverse[0], inverse[1]])
    on_parity(lambda whole, head, tail: (whole.start(), head.start()))
    imag = right_self(1)
    pack_planes(down, [imag], 1)
    pack_tails(down, [real, imag])
    on_parity(lambda whole, head, tail: tail.start())
    on_parity(lambda whole, head, tail: (whole.wait(), head.wait(), tail.wait()))


def group_iotas():
    sublane = lax.broadcasted_iota(jnp.int32, (SUBLANES, LANES), 0)
    lane = lax.broadcasted_iota(jnp.int32, (SUBLANES, LANES), 1)
    return sublane, lane


def along_lanes(values, lanes):
    return jnp.take_along_axis(values, lanes, axis=1, mode="promise_in_bounds")


def table_kernel(
    width, neighbors_ref, phonon_ref, lead_ref, coupling_ref,
    columns_ref, slots_ref, samples_ref, lead_held, coupling_held,
    wide, flat, samples, sems,
):
    fetches = [
        pltpu.make_async_copy(source, held, sems.at[i])
        for i, (source, held) in enumerate(
            ((coupling_ref, coupling_held), (lead_ref, lead_held))
        )
    ]
    for fetch in fetches:
        fetch.start()
    orbitals = neighbors_ref.shape[1]
    groups = orbitals // SUBLANES
    energies = phonon_ref.shape[0]
    sublane, lane = group_iotas()
    own = sublane == lane // width
    wide[...] = jnp.zeros(wide.shape, wide.dtype)
    wide[:, :width] = neighbors_ref[0]
    flat[...] = jnp.full(flat.shape, -1.0, flat.dtype)
    samples[...] = jnp.zeros(samples.shape, samples.dtype)
    tiles = slots_ref.shape[1] // LANES
    for r in range(groups):
        rows = slice(r * SUBLANES, (r + 1) * SUBLANES)
        group = wide[rows, :]
        columns = along_lanes(group, lane % width)
        columns_ref[rows, :] = columns
        flat[r : r + 1, :] = jnp.sum(
            jnp.where(own, columns.astype(jnp.float32), 0.0), axis=0, keepdims=True
        )
        found = [jnp.full((SUBLANES, LANES), -1, jnp.int32) for _ in range(tiles)]
        for k in range(width):
            column = jnp.broadcast_to(group[:, k : k + 1], (SUBLANES, LANES))
            slot = sublane * width + k
            for t in range(tiles):
                found[t] = jnp.where(column == lane + t * LANES, slot, found[t])
        for t in range(tiles):
            slots_ref[rows, t * LANES : (t + 1) * LANES] = found[t]
        for e in range(energies):
            samples[e, :, r, :] = phonon_ref[e, 0, :, r * LANES : (r + 1) * LANES].astype(
                jnp.float32
            )
    for r in range(flat.shape[0] // SUBLANES):
        rows = slice(r * SUBLANES, (r + 1) * SUBLANES)
        here = flat[rows, :]
        values = [[samples[e, c, rows, :] for c in range(2)] for e in range(energies)]
        totals = [list(pair) for pair in values]
        for d in range(1, width):
            turned = (lane // width) * width + (lane + d) % width
            same = here == along_lanes(here, turned)
            for e in range(energies):
                for c in range(2):
                    totals[e][c] = totals[e][c] + jnp.where(
                        same, along_lanes(values[e][c], turned), 0.0
                    )
        for e in range(energies):
            for c in range(2):
                samples[e, c, rows, :] = totals[e][c]
    samples_ref[...] = samples[...].astype(jnp.bfloat16)
    for fetch in fetches:
        fetch.wait()


def unpack_kernel(packed_ref, plane_ref):
    unpack_planes(packed_ref, plane_ref)


def green_kernel(
    width, second_ref, first_planes, lead_ref, inverses_ref, coupling_ref, columns_ref,
    green_ref, pair_ref, previous, right_self, inverse, packed, wide, flat, sems,
):
    orbitals = inverse.shape[1]
    copies = [
        pltpu.make_async_copy(inverses_ref.at[0, 0, c], inverse.at[c], sems.at[c]) for c in range(2)
    ]
    for copy in copies:
        copy.start()
    domain = lax.axis_index("domain")
    even = domain % 2 == 0
    fetch = pltpu.make_async_copy(second_ref, packed, sems.at[2])

    @pl.when(domain > 0)
    def _():
        fetch.start()

    @pl.when(domain == 0)
    def _():
        previous[...] = lead_ref[0]

    @pl.when(even)
    def _():
        right_self[...] = first_planes[...]

    @pl.when(jnp.logical_not(even))
    def _():
        previous[...] = first_planes[...]

    @pl.when(even & (domain > 0))
    def _():
        fetch.wait()
        unpack_planes(packed, previous)

    coupling = coupling_ref[0]
    left_self = []
    for c in range(2):
        left_product = product(previous[c], coupling).astype(jnp.bfloat16)
        left_self.append(product_tn(coupling, left_product).astype(jnp.bfloat16))

    @pl.when(jnp.logical_not(even))
    def _():
        fetch.wait()
        unpack_planes(packed, right_self)

    coupled = [
        (left_self[c].astype(jnp.float32) + right_self[c].astype(jnp.float32)).astype(jnp.bfloat16)
        for c in range(2)
    ]
    for copy in copies:
        copy.wait()
    own = [inverse[c] for c in range(2)]
    inner = [part.astype(jnp.bfloat16) for part in complex_product(coupled, own)]
    for c, part in enumerate(complex_product(own, inner)):
        green = (own[c].astype(jnp.float32) + part).astype(jnp.bfloat16)
        green_ref[c] = green
        wide[c, :, :orbitals] = green.astype(jnp.float32)
    gather_pairs(width, wide, columns_ref, flat, pair_ref, 0)


def sides_kernel(inverses_ref, coupling_ref, before_ref, after_ref, inverse_ref, sems):
    last = inverses_ref.shape[0] - 1
    copies = [
        pltpu.make_async_copy(inverses_ref.at[last, 0, c], inverse_ref.at[c], sems.at[c])
        for c in range(2)
    ]
    for copy in copies:
        copy.start()
    coupling = coupling_ref[0]
    for c in range(2):
        copies[c].wait()
        before_ref[c] = product_nt(inverse_ref[c], coupling).astype(jnp.bfloat16)
        after_ref[c] = product(coupling, inverse_ref[c]).astype(jnp.bfloat16)


def add_side(left, value, middle, right):
    inner = complex_product([middle[c] for c in range(2)], [right[c] for c in range(2)])
    outer = complex_product(
        [left[c] for c in range(2)], [part.astype(jnp.bfloat16) for part in inner]
    )
    return [value[c].astype(jnp.float32) + outer[c] for c in range(2)]


def early_kernel(
    first_ref, lead_ref, before_ref, after_ref, inverse_ref, sum_ref, first_planes
):
    domain = lax.axis_index("domain")
    none = (domain % 2 == 1) & (domain == lax.axis_size("domain") - 1)

    @pl.when((domain > 0) & jnp.logical_not(none))
    def _():
        unpack_planes(first_ref, first_planes)

    def write(values):
        for c in range(2):
            sum_ref[c] = values[c]

    @pl.when(domain == 0)
    def _():
        lead = lead_ref[lead_ref.shape[0] - 1]
        write(add_side(before_ref, inverse_ref, lead, after_ref))

    @pl.when((domain % 2 == 1) & jnp.logical_not(none))
    def _():
        write(add_side(before_ref, inverse_ref, first_planes, after_ref))

    @pl.when((domain % 2 == 0) & (domain > 0))
    def _():
        write(add_side(inverse_ref, inverse_ref, first_planes, inverse_ref))

    @pl.when(none)
    def _():
        write([inverse_ref[c].astype(jnp.float32) for c in range(2)])


def late_kernel(
    width, second_ref, first_ref, before_ref, after_ref, inverse_ref, sum_ref, columns_ref, pair_before,
    green_ref, pair_ref, middle, wide, flat,
):
    orbitals = inverse_ref.shape[1]
    domain = lax.axis_index("domain")
    ends = (domain == 0) | ((domain % 2 == 1) & (domain == lax.axis_size("domain") - 1))

    @pl.when(ends)
    def _():
        unpack_planes(first_ref, middle)

    @pl.when(jnp.logical_not(ends))
    def _():
        unpack_planes(second_ref, middle)

    from_before = (domain > 0) & ((domain % 2 == 0) | ends)

    def write(values):
        for c in range(2):
            green = values[c].astype(jnp.bfloat16)
            green_ref[c] = green
            wide[c, :, :orbitals] = green.astype(jnp.float32)

    @pl.when(from_before)
    def _():
        write(add_side(before_ref, sum_ref, middle, after_ref))

    @pl.when(jnp.logical_not(from_before))
    def _():
        write(add_side(inverse_ref, sum_ref, middle, inverse_ref))

    pair_ref[0] = pair_before[0]
    gather_pairs(width, wide, columns_ref, flat, pair_ref, 1)


def gather_pairs(width, wide, columns_ref, flat, pair_ref, place):
    orbitals = columns_ref.shape[0]
    tiles = wide.shape[2] // LANES
    sublane, lane = group_iotas()
    own = sublane == lane // width
    flat[...] = jnp.zeros(flat.shape, flat.dtype)
    for r in range(orbitals // SUBLANES):
        rows = slice(r * SUBLANES, (r + 1) * SUBLANES)
        columns = columns_ref[rows, :]
        within = columns & (LANES - 1)
        tile = columns // LANES
        for c in range(2):
            taken = jnp.zeros((SUBLANES, LANES), jnp.float32)
            for t in range(tiles):
                candidate = along_lanes(wide[c, rows, t * LANES : (t + 1) * LANES], within)
                taken = jnp.where(own & (tile == t), candidate, taken)
            flat[c, r : r + 1, :] = jnp.sum(taken, axis=0, keepdims=True)
    pair_ref[place] = flat[...].astype(jnp.bfloat16)


def group_kernel(shifts_ref, samples_ref, grouped_ref):
    reach = grouped_ref.shape[0] // 2
    grouped_ref[...] = jnp.zeros(grouped_ref.shape, grouped_ref.dtype)

    def add_point(w, carry):
        place = jnp.clip(shifts_ref[w] + reach, 0, 2 * reach)
        for c in range(2):
            grouped_ref[place, c] = grouped_ref[place, c] + samples_ref[w, c].astype(jnp.float32)
        return carry

    lax.fori_loop(0, samples_ref.shape[0], add_point, 0)


def final_kernel(grouped_ref, slots_ref, green_even_ref, green_odd_ref, *rest):
    *pairs, out_ref, sources, merged, self_block, result, sems = rest
    points = sources.shape[0]
    reach = grouped_ref.shape[0] // 2
    orbitals = result.shape[2]
    groups = orbitals // SUBLANES
    tiles = slots_ref.shape[1] // LANES
    used = merged.shape[2]
    me = lax.axis_index("energy")
    if len(pairs) == 1:

        def widen(p, carry):
            for c in range(2):
                sources[p, c] = pairs[0][p, c].astype(jnp.float32)
            return carry

        lax.fori_loop(0, points, widen, 0, unroll=4)
    else:
        for k, array in enumerate(pairs):
            owner = (me ^ NEAR[k // 2 % 3]) ^ (k % 2)
            for e in range(2):
                for c in range(2):
                    sources[2 * owner + e, c] = array[e, c].astype(jnp.float32)

    def add_shift(place, sums):
        sample = [grouped_ref[place, c, :used, :] for c in range(2)]
        after = []
        for e in range(2):
            source = 2 * me + e + reach - place
            keep = jnp.where((source >= 0) & (source < points), 1.0, 0.0)
            source = jnp.clip(source, 0, points - 1)
            real, imag = (sources[source, c, :used, :] for c in range(2))
            after.append(
                (
                    sums[e][0] + keep * (sample[0] * real - sample[1] * imag),
                    sums[e][1] + keep * (sample[0] * imag + sample[1] * real),
                )
            )
        return tuple(after)

    zero = jnp.zeros((used, LANES), jnp.float32)
    sums = lax.fori_loop(0, 2 * reach + 1, add_shift, ((zero, zero), (zero, zero)), unroll=3)
    for e in range(2):
        for c in range(2):
            merged[e, c] = sums[e][c]
    copies = []
    for e, green_ref in enumerate((green_even_ref, green_odd_ref)):
        for q in range(groups // 2):
            for t in range(tiles):
                found = [[], []]
                for r in (2 * q, 2 * q + 1):
                    slot = slots_ref[r * SUBLANES : (r + 1) * SUBLANES, t * LANES : (t + 1) * LANES]
                    within = slot & (LANES - 1)
                    for c in range(2):
                        row = jnp.broadcast_to(merged[e, c, r : r + 1, :], (SUBLANES, LANES))
                        found[c].append(jnp.where(slot >= 0, along_lanes(row, within), 0.0))
                for c in range(2):
                    self_block[e, c, q * 16 : (q + 1) * 16, t * LANES : (t + 1) * LANES] = (
                        jnp.concatenate(found[c], axis=0).astype(jnp.bfloat16)
                    )
    for e, green_ref in enumerate((green_even_ref, green_odd_ref)):
        green = [green_ref[c] for c in range(2)]
        sigma = [self_block[e, c, :, :orbitals] for c in range(2)]
        scattered = [part.astype(jnp.bfloat16) for part in complex_product(green, sigma)]
        reals = product(scattered[0], green[0])
        imags = product(scattered[1], green[1])

        def put(c, part):
            result[e, c] = (green[c].astype(jnp.float32) + part).astype(jnp.bfloat16)
            copies.append(pltpu.make_async_copy(result.at[e, c], out_ref.at[e, 0, c], sems.at[e, c]))
            copies[-1].start()

        put(0, reals - imags)
        put(1, product(scattered[0] + scattered[1], green[0] + green[1]) - reals - imags)
    for copy in copies:
        copy.wait()


IN_VMEM = pl.BlockSpec(memory_space=pltpu.VMEM)
IN_SMEM = pl.BlockSpec(memory_space=pltpu.SMEM)
IN_HBM = pl.BlockSpec(memory_space=pltpu.HBM)


def call(kernel, out_shape, in_specs, scratch=(), flops=0, bytes_accessed=1 << 20, out_spec=None, limit=4):
    return pl.pallas_call(
        kernel,
        out_shape=out_shape,
        in_specs=in_specs,
        out_specs=out_spec or (IN_VMEM if not isinstance(out_shape, tuple) else (IN_VMEM,) * len(out_shape)),
        scratch_shapes=list(scratch),
        compiler_params=pltpu.CompilerParams(vmem_limit_bytes=limit * MIB),
        cost_estimate=pl.CostEstimate(flops=flops, bytes_accessed=bytes_accessed, transcendentals=0),
    )


def body(inverses, coupling, lead_green, phonon, neighbors, shifts):
    energies = inverses.shape[0]
    orbitals = inverses.shape[3]
    width = neighbors.shape[2]
    points = shifts.shape[0]
    rows = packed_rows(orbitals)
    groups = orbitals * width // LANES
    used = -(-groups // SUBLANES) * SUBLANES
    height = -(-groups // 16) * 16
    padded = -(-orbitals // LANES) * LANES
    bf16, f32 = jnp.bfloat16, jnp.float32
    shape = jax.ShapeDtypeStruct
    cube = 2 * orbitals**3
    plane = (orbitals, orbitals)
    domains = lax.axis_size("domain")
    routes = [
        [swap for i in range(start, domains - 1, 2) for swap in ((i, i + 1), (i + 1, i))]
        for start in range(2)
    ]

    in_hbm = [
        pltpu.with_memory_space_constraint(array, pltpu.HBM)
        for array in (inverses, coupling, lead_green)
    ]

    barred = in_hbm[0]
    received = []
    for e in range(energies):
        sent = call(
            functools.partial(send_kernel, e),
            (shape((rows, LANES), bf16), shape((rows, LANES), bf16)),
            [IN_HBM] * 2,
            [
                pltpu.VMEM((2, *plane), bf16),
                pltpu.VMEM(plane, bf16),
                pltpu.VMEM((rows, LANES), bf16),
                pltpu.VMEM((rows, LANES), bf16),
                pltpu.SemaphoreType.DMA((3,)),
                pltpu.SemaphoreType.DMA,
                pltpu.SemaphoreType.DMA((2,)),
            ],
            flops=4 * cube,
            out_spec=(IN_HBM,) * 2,
        )(barred, in_hbm[1])
        received.append([lax.ppermute(x, "domain", route) for x, route in zip(sent, routes)])
        barred, neighbors, _ = lax.optimization_barrier((barred, neighbors, sent[0]))
        barred = pltpu.with_memory_space_constraint(barred, pltpu.HBM)
    columns, slots, samples, lead, coupling = call(
        functools.partial(table_kernel, width),
        (
            shape((orbitals, LANES), jnp.int32),
            shape((orbitals, padded), jnp.int32),
            shape((energies, 2, height, LANES), bf16),
            pltpu.VMEM(lead_green.shape, bf16),
            pltpu.VMEM(coupling.shape, bf16),
        ),
        [IN_VMEM, IN_VMEM, IN_HBM, IN_HBM],
        [
            pltpu.VMEM((orbitals, LANES), jnp.int32),
            pltpu.VMEM((height, LANES), f32),
            pltpu.VMEM((energies, 2, height, LANES), f32),
            pltpu.SemaphoreType.DMA((2,)),
        ],
        flops=4 * cube,
    )(neighbors, phonon, in_hbm[2], in_hbm[1])
    samples = lax.all_gather(samples, "energy", axis=0, tiled=True)
    columns, samples = lax.optimization_barrier((columns, samples))

    pair_shape = (1, 2, height, LANES)
    block = shape((2, *plane), bf16)
    before, after, inverse = call(
        sides_kernel,
        (block,) * 3,
        [IN_HBM, IN_VMEM],
        [pltpu.SemaphoreType.DMA((2,))],
        flops=4 * cube,
    )(in_hbm[0], coupling)

    def unpacked(first):
        return call(unpack_kernel, block, [IN_VMEM])(first)

    first, second = received[0]
    green_even, pair = call(
        functools.partial(green_kernel, width),
        (block, shape(pair_shape, bf16)),
        [IN_HBM] + [IN_VMEM] * 2 + [IN_HBM] + [IN_VMEM] * 2,
        [
            pltpu.VMEM((2, *plane), bf16),
            pltpu.VMEM((2, *plane), bf16),
            pltpu.VMEM((2, *plane), bf16),
            pltpu.VMEM((rows, LANES), bf16),
            pltpu.VMEM((2, orbitals, padded), f32),
            pltpu.VMEM((2, height, LANES), f32),
            pltpu.SemaphoreType.DMA((3,)),
        ],
        flops=12 * cube,
        limit=12,
    )(pltpu.with_memory_space_constraint(second, pltpu.HBM), unpacked(first), lead, in_hbm[0], coupling, columns)

    reach = points // 4
    grouped = call(
        group_kernel, shape((2 * reach + 1, 2, height, LANES), f32), [IN_SMEM, IN_VMEM]
    )(shifts, samples)

    first, second = received[1]
    first, pair, grouped = lax.optimization_barrier((first, pair, grouped))
    partial_sum = call(
        early_kernel,
        shape((2, *plane), f32),
        [IN_VMEM] * 5,
        [pltpu.VMEM((2, *plane), bf16)],
        flops=6 * cube,
        limit=12,
    )(first, lead, before, after, inverse)
    green_odd, pair = call(
        functools.partial(late_kernel, width),
        (block, shape((2, *pair_shape[1:]), bf16)),
        [IN_VMEM] * 8,
        [
            pltpu.VMEM((2, *plane), bf16),
            pltpu.VMEM((2, orbitals, padded), f32),
            pltpu.VMEM((2, height, LANES), f32),
        ],
        flops=6 * cube,
        limit=12,
    )(second, first, before, after, inverse, partial_sum, columns, pair)
    devices = lax.axis_size("energy")
    if devices == 8 and energies == 2:
        across = lax.ppermute(pair, "energy", [(i, i ^ 6) for i in range(2, 6)])
        beside = lax.ppermute(pair, "energy", [(i, i ^ 2) for i in range(8)])
        sources = []
        for array in (pair, beside, across):
            sources += [array, lax.ppermute(array, "energy", [(i, i ^ 1) for i in range(8)])]
    else:
        sources = [lax.all_gather(pair, "energy", axis=0, tiled=True)]

    return call(
        final_kernel,
        shape((energies, 1, 2, *plane), bf16),
        [IN_VMEM] * (4 + len(sources)),
        [
            pltpu.VMEM((points, 2, height, LANES), f32),
            pltpu.VMEM((2, 2, used, LANES), f32),
            pltpu.VMEM((2, 2, orbitals, padded), bf16),
            pltpu.VMEM((2, 2, *plane), bf16),
            pltpu.SemaphoreType.DMA((2, 2)),
        ],
        flops=16 * cube,
        out_spec=IN_HBM,
        limit=16,
    )(grouped, slots, green_even, green_odd, *sources)


def solution(mesh):
    return jax.shard_map(
        body,
        mesh=mesh,
        in_specs=(
            P("energy", "domain", None, None, None),
            P("domain", None, None),
            P("energy", None, None, None),
            P("energy", "domain", None, None),
            P("domain", None, None),
            P(),
        ),
        out_specs=P("energy", "domain", None, None, None),
        check_vma=False,
    )
```

```python
import functools

import jax
import jax.numpy as jnp
from jax import lax
from jax.experimental import pallas as pl
from jax.experimental.pallas import tpu as pltpu
from jax.sharding import PartitionSpec as P

LANES = 128
NEAR = (0, 6, 2)
SUBLANES = 8
MIB = 1024 * 1024


def product(first, second):
    return jnp.dot(first, second, preferred_element_type=jnp.float32)


def product_nt(first, second):
    return lax.dot_general(
        first, second, (((1,), (1,)), ((), ())), preferred_element_type=jnp.float32
    )


def product_tn(first, second):
    return lax.dot_general(
        first, second, (((0,), (0,)), ((), ())), preferred_element_type=jnp.float32
    )


def complex_product(first, second):
    reals = product(first[0], second[0])
    imags = product(first[1], second[1])
    both = product(first[0] + first[1], second[0] + second[1])
    return reals - imags, both - reals - imags


def packed_rows(orbitals):
    return 2 * orbitals * orbitals // LANES


def pack_planes(out_ref, planes, place):
    orbitals = planes[0].shape[0]
    whole = orbitals // LANES
    for c, plane in enumerate(planes, place):
        for t in range(whole):
            out_ref[pl.ds((c * whole + t) * orbitals, orbitals), :] = plane[
                :, t * LANES : (t + 1) * LANES
            ]


def pack_tails(out_ref, planes):
    orbitals = planes[0].shape[0]
    whole = orbitals // LANES
    rest = orbitals - whole * LANES
    pieces = LANES // rest // 2
    height = orbitals // pieces
    tails = [
        plane[h * height : (h + 1) * height, whole * LANES :]
        for plane in planes
        for h in range(pieces)
    ]
    out_ref[pl.ds(2 * whole * orbitals, height), :] = jnp.concatenate(tails, axis=1)


def unpack_planes(packed_ref, plane_ref):
    orbitals = plane_ref.shape[1]
    whole = orbitals // LANES
    rest = orbitals - whole * LANES
    pieces = LANES // rest // 2
    height = orbitals // pieces
    tails = packed_ref[pl.ds(2 * whole * orbitals, height), :]
    for c in range(2):
        for t in range(whole):
            plane_ref[c, :, t * LANES : (t + 1) * LANES] = packed_ref[
                pl.ds((c * whole + t) * orbitals, orbitals), :
            ]
        for h in range(pieces):
            start = (c * pieces + h) * rest
            plane_ref[c, h * height : (h + 1) * height, whole * LANES :] = tails[
                :, start : start + rest
            ]


def send_kernel(
    e, inverses_ref, coupling_ref, first_ref, second_ref,
    inverse, coupling, up, down, sems, up_sem, down_sems,
):
    copies = [pltpu.make_async_copy(coupling_ref.at[0], coupling, sems.at[2])]
    for c in range(2):
        copies.append(pltpu.make_async_copy(inverses_ref.at[e, 0, c], inverse.at[c], sems.at[c]))
    for copy in copies:
        copy.start()
    even = lax.axis_index("domain") % 2 == 0
    split = inverse.shape[1] * (inverse.shape[2] // LANES)

    def on_parity(act):
        for parity, next_ref, before_ref in ((True, first_ref, second_ref), (False, second_ref, first_ref)):

            @pl.when(even == parity)
            def _():
                act(
                    pltpu.make_async_copy(up, next_ref, up_sem),
                    pltpu.make_async_copy(
                        down.at[pl.ds(0, split)], before_ref.at[pl.ds(0, split)], down_sems.at[0]
                    ),
                    pltpu.make_async_copy(
                        down.at[pl.ds(split, down.shape[0] - split)],
                        before_ref.at[pl.ds(split, down.shape[0] - split)],
                        down_sems.at[1],
                    ),
                )

    def right_self(c):
        right_product = product_nt(inverse[c], coupling[...]).astype(jnp.bfloat16)
        return product(coupling[...], right_product).astype(jnp.bfloat16)

    copies[0].wait()
    copies[1].wait()
    real = right_self(0)
    pack_planes(down, [real], 0)
    copies[2].wait()
    pack_planes(up, [inverse[0], inverse[1]], 0)
    pack_tails(up, [inverse[0], inverse[1]])
    on_parity(lambda whole, head, tail: (whole.start(), head.start()))
    imag = right_self(1)
    pack_planes(down, [imag], 1)
    pack_tails(down, [real, imag])
    on_parity(lambda whole, head, tail: tail.start())
    on_parity(lambda whole, head, tail: (whole.wait(), head.wait(), tail.wait()))


def group_iotas():
    sublane = lax.broadcasted_iota(jnp.int32, (SUBLANES, LANES), 0)
    lane = lax.broadcasted_iota(jnp.int32, (SUBLANES, LANES), 1)
    return sublane, lane


def along_lanes(values, lanes):
    return jnp.take_along_axis(values, lanes, axis=1, mode="promise_in_bounds")


def table_kernel(
    width, neighbors_ref, phonon_ref, lead_ref, coupling_ref,
    columns_ref, slots_ref, samples_ref, lead_held, coupling_held,
    wide, flat, samples, sems,
):
    fetches = [
        pltpu.make_async_copy(source, held, sems.at[i])
        for i, (source, held) in enumerate(
            ((coupling_ref, coupling_held), (lead_ref, lead_held))
        )
    ]
    for fetch in fetches:
        fetch.start()
    orbitals = neighbors_ref.shape[1]
    groups = orbitals // SUBLANES
    energies = phonon_ref.shape[0]
    sublane, lane = group_iotas()
    own = sublane == lane // width
    wide[...] = jnp.zeros(wide.shape, wide.dtype)
    wide[:, :width] = neighbors_ref[0]
    flat[...] = jnp.full(flat.shape, -1.0, flat.dtype)
    samples[...] = jnp.zeros(samples.shape, samples.dtype)
    tiles = slots_ref.shape[1] // LANES
    for r in range(groups):
        rows = slice(r * SUBLANES, (r + 1) * SUBLANES)
        group = wide[rows, :]
        columns = along_lanes(group, lane % width)
        columns_ref[rows, :] = columns
        flat[r : r + 1, :] = jnp.sum(
            jnp.where(own, columns.astype(jnp.float32), 0.0), axis=0, keepdims=True
        )
        found = [jnp.full((SUBLANES, LANES), -1, jnp.int32) for _ in range(tiles)]
        for k in range(width):
            column = jnp.broadcast_to(group[:, k : k + 1], (SUBLANES, LANES))
            slot = sublane * width + k
            for t in range(tiles):
                found[t] = jnp.where(column == lane + t * LANES, slot, found[t])
        for t in range(tiles):
            slots_ref[rows, t * LANES : (t + 1) * LANES] = found[t]
        for e in range(energies):
            samples[e, :, r, :] = phonon_ref[e, 0, :, r * LANES : (r + 1) * LANES].astype(
                jnp.float32
            )
    for r in range(flat.shape[0] // SUBLANES):
        rows = slice(r * SUBLANES, (r + 1) * SUBLANES)
        here = flat[rows, :]
        values = [[samples[e, c, rows, :] for c in range(2)] for e in range(energies)]
        totals = [list(pair) for pair in values]
        for d in range(1, width):
            turned = (lane // width) * width + (lane + d) % width
            same = here == along_lanes(here, turned)
            for e in range(energies):
                for c in range(2):
                    totals[e][c] = totals[e][c] + jnp.where(
                        same, along_lanes(values[e][c], turned), 0.0
                    )
        for e in range(energies):
            for c in range(2):
                samples[e, c, rows, :] = totals[e][c]
    samples_ref[...] = samples[...].astype(jnp.bfloat16)
    for fetch in fetches:
        fetch.wait()


def unpack_kernel(packed_ref, plane_ref):
    unpack_planes(packed_ref, plane_ref)


def green_kernel(
    width, second_ref, first_planes, lead_ref, inverse_ref, coupling_ref, columns_ref,
    green_ref, pair_ref, previous, right_self, wide, flat,
):
    orbitals = inverse_ref.shape[1]
    domain = lax.axis_index("domain")
    even = domain % 2 == 0

    @pl.when(domain == 0)
    def _():
        previous[...] = lead_ref[0]

    @pl.when(even & (domain > 0))
    def _():
        unpack_planes(second_ref, previous)

    @pl.when(even)
    def _():
        right_self[...] = first_planes[...]

    @pl.when(jnp.logical_not(even))
    def _():
        previous[...] = first_planes[...]
        unpack_planes(second_ref, right_self)

    coupling = coupling_ref[0]
    coupled = []
    for c in range(2):
        left_product = product(previous[c], coupling).astype(jnp.bfloat16)
        left_self = product_tn(coupling, left_product).astype(jnp.bfloat16)
        coupled.append(
            (left_self.astype(jnp.float32) + right_self[c].astype(jnp.float32)).astype(jnp.bfloat16)
        )
    own = [inverse_ref[c] for c in range(2)]
    inner = [part.astype(jnp.bfloat16) for part in complex_product(coupled, own)]
    for c, part in enumerate(complex_product(own, inner)):
        green = (own[c].astype(jnp.float32) + part).astype(jnp.bfloat16)
        green_ref[c] = green
        wide[c, :, :orbitals] = green.astype(jnp.float32)
    gather_pairs(width, wide, columns_ref, flat, pair_ref, 0)


def sides_kernel(
    inverses_ref, second_ref, coupling_ref, before_ref, after_ref, inverse_ref, first_inverse, packed, sems
):
    last = inverses_ref.shape[0] - 1
    copies = [
        pltpu.make_async_copy(inverses_ref.at[e, 0, c], held.at[c], sems.at[k, c])
        for k, (e, held) in enumerate(((last, inverse_ref), (0, first_inverse)))
        for c in range(2)
    ]
    copies.append(pltpu.make_async_copy(second_ref, packed, sems.at[2, 0]))
    for copy in copies:
        copy.start()
    coupling = coupling_ref[0]
    for c in range(2):
        copies[c].wait()
        before_ref[c] = product_nt(inverse_ref[c], coupling).astype(jnp.bfloat16)
        after_ref[c] = product(coupling, inverse_ref[c]).astype(jnp.bfloat16)
    for copy in copies[2:]:
        copy.wait()


def add_side(left, value, middle, right):
    inner = complex_product([middle[c] for c in range(2)], [right[c] for c in range(2)])
    outer = complex_product(
        [left[c] for c in range(2)], [part.astype(jnp.bfloat16) for part in inner]
    )
    return [value[c].astype(jnp.float32) + outer[c] for c in range(2)]


def early_kernel(
    first_ref, lead_ref, before_ref, after_ref, inverse_ref, sum_ref, first_planes
):
    domain = lax.axis_index("domain")
    none = (domain % 2 == 1) & (domain == lax.axis_size("domain") - 1)

    @pl.when((domain > 0) & jnp.logical_not(none))
    def _():
        unpack_planes(first_ref, first_planes)

    def write(values):
        for c in range(2):
            sum_ref[c] = values[c]

    @pl.when(domain == 0)
    def _():
        lead = lead_ref[lead_ref.shape[0] - 1]
        write(add_side(before_ref, inverse_ref, lead, after_ref))

    @pl.when((domain % 2 == 1) & jnp.logical_not(none))
    def _():
        write(add_side(before_ref, inverse_ref, first_planes, after_ref))

    @pl.when((domain % 2 == 0) & (domain > 0))
    def _():
        write(add_side(inverse_ref, inverse_ref, first_planes, inverse_ref))

    @pl.when(none)
    def _():
        write([inverse_ref[c].astype(jnp.float32) for c in range(2)])


def late_kernel(
    width, second_ref, first_ref, before_ref, after_ref, inverse_ref, sum_ref, columns_ref, pair_before,
    green_ref, pair_ref, middle, wide, flat,
):
    orbitals = inverse_ref.shape[1]
    domain = lax.axis_index("domain")
    ends = (domain == 0) | ((domain % 2 == 1) & (domain == lax.axis_size("domain") - 1))

    @pl.when(ends)
    def _():
        unpack_planes(first_ref, middle)

    @pl.when(jnp.logical_not(ends))
    def _():
        unpack_planes(second_ref, middle)

    from_before = (domain > 0) & ((domain % 2 == 0) | ends)

    def write(values):
        for c in range(2):
            green = values[c].astype(jnp.bfloat16)
            green_ref[c] = green
            wide[c, :, :orbitals] = green.astype(jnp.float32)

    @pl.when(from_before)
    def _():
        write(add_side(before_ref, sum_ref, middle, after_ref))

    @pl.when(jnp.logical_not(from_before))
    def _():
        write(add_side(inverse_ref, sum_ref, middle, inverse_ref))

    pair_ref[0] = pair_before[0]
    gather_pairs(width, wide, columns_ref, flat, pair_ref, 1)


def gather_pairs(width, wide, columns_ref, flat, pair_ref, place):
    orbitals = columns_ref.shape[0]
    tiles = wide.shape[2] // LANES
    sublane, lane = group_iotas()
    own = sublane == lane // width
    flat[...] = jnp.zeros(flat.shape, flat.dtype)
    for r in range(orbitals // SUBLANES):
        rows = slice(r * SUBLANES, (r + 1) * SUBLANES)
        columns = columns_ref[rows, :]
        within = columns & (LANES - 1)
        tile = columns // LANES
        for c in range(2):
            taken = jnp.zeros((SUBLANES, LANES), jnp.float32)
            for t in range(tiles):
                candidate = along_lanes(wide[c, rows, t * LANES : (t + 1) * LANES], within)
                taken = jnp.where(own & (tile == t), candidate, taken)
            flat[c, r : r + 1, :] = jnp.sum(taken, axis=0, keepdims=True)
    pair_ref[place] = flat[...].astype(jnp.bfloat16)


def group_kernel(shifts_ref, samples_ref, grouped_ref):
    reach = grouped_ref.shape[0] // 2
    grouped_ref[...] = jnp.zeros(grouped_ref.shape, grouped_ref.dtype)

    def add_point(w, carry):
        place = jnp.clip(shifts_ref[w] + reach, 0, 2 * reach)
        for c in range(2):
            grouped_ref[place, c] = grouped_ref[place, c] + samples_ref[w, c].astype(jnp.float32)
        return carry

    lax.fori_loop(0, samples_ref.shape[0], add_point, 0)


def final_kernel(grouped_ref, slots_ref, green_even_ref, green_odd_ref, *rest):
    *pairs, out_ref, sources, merged, self_block, result, sems = rest
    points = sources.shape[0]
    reach = grouped_ref.shape[0] // 2
    orbitals = result.shape[2]
    groups = orbitals // SUBLANES
    tiles = slots_ref.shape[1] // LANES
    used = merged.shape[2]
    me = lax.axis_index("energy")
    if len(pairs) == 1:

        def widen(p, carry):
            for c in range(2):
                sources[p, c] = pairs[0][p, c].astype(jnp.float32)
            return carry

        lax.fori_loop(0, points, widen, 0, unroll=4)
    else:
        for k, array in enumerate(pairs):
            owner = (me ^ NEAR[k // 2 % 3]) ^ (k % 2)
            for e in range(2):
                for c in range(2):
                    sources[2 * owner + e, c] = array[e, c].astype(jnp.float32)

    def add_shift(place, sums):
        sample = [grouped_ref[place, c, :used, :] for c in range(2)]
        after = []
        for e in range(2):
            source = 2 * me + e + reach - place
            keep = jnp.where((source >= 0) & (source < points), 1.0, 0.0)
            source = jnp.clip(source, 0, points - 1)
            real, imag = (sources[source, c, :used, :] for c in range(2))
            after.append(
                (
                    sums[e][0] + keep * (sample[0] * real - sample[1] * imag),
                    sums[e][1] + keep * (sample[0] * imag + sample[1] * real),
                )
            )
        return tuple(after)

    zero = jnp.zeros((used, LANES), jnp.float32)
    sums = lax.fori_loop(0, 2 * reach + 1, add_shift, ((zero, zero), (zero, zero)), unroll=3)
    for e in range(2):
        for c in range(2):
            merged[e, c] = sums[e][c]
    copies = []
    for e, green_ref in enumerate((green_even_ref, green_odd_ref)):
        for q in range(groups // 2):
            for t in range(tiles):
                found = [[], []]
                for r in (2 * q, 2 * q + 1):
                    slot = slots_ref[r * SUBLANES : (r + 1) * SUBLANES, t * LANES : (t + 1) * LANES]
                    within = slot & (LANES - 1)
                    for c in range(2):
                        row = jnp.broadcast_to(merged[e, c, r : r + 1, :], (SUBLANES, LANES))
                        found[c].append(jnp.where(slot >= 0, along_lanes(row, within), 0.0))
                for c in range(2):
                    self_block[e, c, q * 16 : (q + 1) * 16, t * LANES : (t + 1) * LANES] = (
                        jnp.concatenate(found[c], axis=0).astype(jnp.bfloat16)
                    )
    for e, green_ref in enumerate((green_even_ref, green_odd_ref)):
        green = [green_ref[c] for c in range(2)]
        sigma = [self_block[e, c, :, :orbitals] for c in range(2)]
        scattered = [part.astype(jnp.bfloat16) for part in complex_product(green, sigma)]
        reals = product(scattered[0], green[0])
        imags = product(scattered[1], green[1])

        def put(c, part):
            result[e, c] = (green[c].astype(jnp.float32) + part).astype(jnp.bfloat16)
            copies.append(pltpu.make_async_copy(result.at[e, c], out_ref.at[e, 0, c], sems.at[e, c]))
            copies[-1].start()

        put(0, reals - imags)
        put(1, product(scattered[0] + scattered[1], green[0] + green[1]) - reals - imags)
    for copy in copies:
        copy.wait()


IN_VMEM = pl.BlockSpec(memory_space=pltpu.VMEM)
IN_SMEM = pl.BlockSpec(memory_space=pltpu.SMEM)
IN_HBM = pl.BlockSpec(memory_space=pltpu.HBM)


def call(kernel, out_shape, in_specs, scratch=(), flops=0, bytes_accessed=1 << 20, out_spec=None, limit=4):
    return pl.pallas_call(
        kernel,
        out_shape=out_shape,
        in_specs=in_specs,
        out_specs=out_spec or (IN_VMEM if not isinstance(out_shape, tuple) else (IN_VMEM,) * len(out_shape)),
        scratch_shapes=list(scratch),
        compiler_params=pltpu.CompilerParams(vmem_limit_bytes=limit * MIB),
        cost_estimate=pl.CostEstimate(flops=flops, bytes_accessed=bytes_accessed, transcendentals=0),
    )


def body(inverses, coupling, lead_green, phonon, neighbors, shifts):
    energies = inverses.shape[0]
    orbitals = inverses.shape[3]
    width = neighbors.shape[2]
    points = shifts.shape[0]
    rows = packed_rows(orbitals)
    groups = orbitals * width // LANES
    used = -(-groups // SUBLANES) * SUBLANES
    height = -(-groups // 16) * 16
    padded = -(-orbitals // LANES) * LANES
    bf16, f32 = jnp.bfloat16, jnp.float32
    shape = jax.ShapeDtypeStruct
    cube = 2 * orbitals**3
    plane = (orbitals, orbitals)
    domains = lax.axis_size("domain")
    routes = [
        [swap for i in range(start, domains - 1, 2) for swap in ((i, i + 1), (i + 1, i))]
        for start in range(2)
    ]

    in_hbm = [
        pltpu.with_memory_space_constraint(array, pltpu.HBM)
        for array in (inverses, coupling, lead_green)
    ]

    barred = in_hbm[0]
    received = []
    for e in range(energies):
        sent = call(
            functools.partial(send_kernel, e),
            (shape((rows, LANES), bf16), shape((rows, LANES), bf16)),
            [IN_HBM] * 2,
            [
                pltpu.VMEM((2, *plane), bf16),
                pltpu.VMEM(plane, bf16),
                pltpu.VMEM((rows, LANES), bf16),
                pltpu.VMEM((rows, LANES), bf16),
                pltpu.SemaphoreType.DMA((3,)),
                pltpu.SemaphoreType.DMA,
                pltpu.SemaphoreType.DMA((2,)),
            ],
            flops=4 * cube,
            out_spec=(IN_HBM,) * 2,
        )(barred, in_hbm[1])
        received.append([lax.ppermute(x, "domain", route) for x, route in zip(sent, routes)])
        barred, neighbors, _ = lax.optimization_barrier((barred, neighbors, sent[0]))
        barred = pltpu.with_memory_space_constraint(barred, pltpu.HBM)
    columns, slots, samples, lead, coupling = call(
        functools.partial(table_kernel, width),
        (
            shape((orbitals, LANES), jnp.int32),
            shape((orbitals, padded), jnp.int32),
            shape((energies, 2, height, LANES), bf16),
            pltpu.VMEM(lead_green.shape, bf16),
            pltpu.VMEM(coupling.shape, bf16),
        ),
        [IN_VMEM, IN_VMEM, IN_HBM, IN_HBM],
        [
            pltpu.VMEM((orbitals, LANES), jnp.int32),
            pltpu.VMEM((height, LANES), f32),
            pltpu.VMEM((energies, 2, height, LANES), f32),
            pltpu.SemaphoreType.DMA((2,)),
        ],
        flops=4 * cube,
    )(neighbors, phonon, in_hbm[2], in_hbm[1])
    samples = lax.all_gather(samples, "energy", axis=0, tiled=True)
    columns, samples = lax.optimization_barrier((columns, samples))

    pair_shape = (1, 2, height, LANES)
    block = shape((2, *plane), bf16)

    def unpacked(first):
        return call(unpack_kernel, block, [IN_VMEM])(first)

    first, second = received[0]
    first, second = lax.optimization_barrier((unpacked(first), second))
    before, after, inverse, first_inverse, second = call(
        sides_kernel,
        (*(block,) * 4, shape((rows, LANES), bf16)),
        [IN_HBM, IN_HBM, IN_VMEM],
        [pltpu.SemaphoreType.DMA((3, 2))],
        flops=4 * cube,
    )(in_hbm[0], pltpu.with_memory_space_constraint(second, pltpu.HBM), coupling)
    green_even, pair = call(
        functools.partial(green_kernel, width),
        (block, shape(pair_shape, bf16)),
        [IN_VMEM] * 6,
        [
            pltpu.VMEM((2, *plane), bf16),
            pltpu.VMEM((2, *plane), bf16),
            pltpu.VMEM((2, orbitals, padded), f32),
            pltpu.VMEM((2, height, LANES), f32),
        ],
        flops=12 * cube,
        limit=12,
    )(second, first, lead, first_inverse, coupling, columns)

    reach = points // 4
    grouped = call(
        group_kernel, shape((2 * reach + 1, 2, height, LANES), f32), [IN_SMEM, IN_VMEM]
    )(shifts, samples)

    first, second = received[1]
    first, pair, grouped = lax.optimization_barrier((first, pair, grouped))
    partial_sum = call(
        early_kernel,
        shape((2, *plane), f32),
        [IN_VMEM] * 5,
        [pltpu.VMEM((2, *plane), bf16)],
        flops=6 * cube,
        limit=12,
    )(first, lead, before, after, inverse)
    green_odd, pair = call(
        functools.partial(late_kernel, width),
        (block, shape((2, *pair_shape[1:]), bf16)),
        [IN_VMEM] * 8,
        [
            pltpu.VMEM((2, *plane), bf16),
            pltpu.VMEM((2, orbitals, padded), f32),
            pltpu.VMEM((2, height, LANES), f32),
        ],
        flops=6 * cube,
        limit=12,
    )(second, first, before, after, inverse, partial_sum, columns, pair)
    devices = lax.axis_size("energy")
    if devices == 8 and energies == 2:
        swap = [(i, i ^ 1) for i in range(devices)]
        beside = lax.ppermute(pair, "energy", [(i, i ^ 2) for i in range(devices)])
        across = lax.ppermute(pair, "energy", [(i, i ^ 6) for i in range(2, 6)])
        sources = []
        for array in (pair, across, beside):
            sources += [array, lax.ppermute(array, "energy", swap)]
    else:
        sources = [lax.all_gather(pair, "energy", axis=0, tiled=True)]

    return call(
        final_kernel,
        shape((energies, 1, 2, *plane), bf16),
        [IN_VMEM] * (4 + len(sources)),
        [
            pltpu.VMEM((points, 2, height, LANES), f32),
            pltpu.VMEM((2, 2, used, LANES), f32),
            pltpu.VMEM((2, 2, orbitals, padded), bf16),
            pltpu.VMEM((2, 2, *plane), bf16),
            pltpu.SemaphoreType.DMA((2, 2)),
        ],
        flops=16 * cube,
        out_spec=IN_HBM,
        limit=16,
    )(grouped, slots, green_even, green_odd, *sources)


def solution(mesh):
    return jax.shard_map(
        body,
        mesh=mesh,
        in_specs=(
            P("energy", "domain", None, None, None),
            P("domain", None, None),
            P("energy", None, None, None),
            P("energy", "domain", None, None),
            P("domain", None, None),
            P(),
        ),
        out_specs=P("energy", "domain", None, None, None),
        check_vma=False,
    )
```

```python
import functools

import jax
import jax.numpy as jnp
from jax import lax
from jax.experimental import pallas as pl
from jax.experimental.pallas import tpu as pltpu
from jax.sharding import PartitionSpec as P

LANES = 128
NEAR = (0, 6, 2)
SUBLANES = 8
MIB = 1024 * 1024


def product(first, second):
    return jnp.dot(first, second, preferred_element_type=jnp.float32)


def product_nt(first, second):
    return lax.dot_general(
        first, second, (((1,), (1,)), ((), ())), preferred_element_type=jnp.float32
    )


def product_tn(first, second):
    return lax.dot_general(
        first, second, (((0,), (0,)), ((), ())), preferred_element_type=jnp.float32
    )


def complex_product(first, second):
    reals = product(first[0], second[0])
    imags = product(first[1], second[1])
    both = product(first[0] + first[1], second[0] + second[1])
    return reals - imags, both - reals - imags


def packed_rows(orbitals):
    return 2 * orbitals * orbitals // LANES


def pack_planes(out_ref, planes, place):
    orbitals = planes[0].shape[0]
    whole = orbitals // LANES
    for c, plane in enumerate(planes, place):
        for t in range(whole):
            out_ref[pl.ds((c * whole + t) * orbitals, orbitals), :] = plane[
                :, t * LANES : (t + 1) * LANES
            ]


def pack_tails(out_ref, planes):
    orbitals = planes[0].shape[0]
    whole = orbitals // LANES
    rest = orbitals - whole * LANES
    pieces = LANES // rest // 2
    height = orbitals // pieces
    tails = [
        plane[h * height : (h + 1) * height, whole * LANES :]
        for plane in planes
        for h in range(pieces)
    ]
    out_ref[pl.ds(2 * whole * orbitals, height), :] = jnp.concatenate(tails, axis=1)


def unpack_planes(packed_ref, plane_ref):
    orbitals = plane_ref.shape[1]
    whole = orbitals // LANES
    rest = orbitals - whole * LANES
    pieces = LANES // rest // 2
    height = orbitals // pieces
    tails = packed_ref[pl.ds(2 * whole * orbitals, height), :]
    for c in range(2):
        for t in range(whole):
            plane_ref[c, :, t * LANES : (t + 1) * LANES] = packed_ref[
                pl.ds((c * whole + t) * orbitals, orbitals), :
            ]
        for h in range(pieces):
            start = (c * pieces + h) * rest
            plane_ref[c, h * height : (h + 1) * height, whole * LANES :] = tails[
                :, start : start + rest
            ]


def send_kernel(
    e, inverses_ref, coupling_ref, first_ref, second_ref,
    inverse, coupling, up, down, sems, up_sem, down_sems,
):
    copies = [pltpu.make_async_copy(coupling_ref.at[0], coupling, sems.at[2])]
    for c in range(2):
        copies.append(pltpu.make_async_copy(inverses_ref.at[e, 0, c], inverse.at[c], sems.at[c]))
    for copy in copies:
        copy.start()
    even = lax.axis_index("domain") % 2 == 0
    split = inverse.shape[1] * (inverse.shape[2] // LANES)

    def on_parity(act):
        for parity, next_ref, before_ref in ((True, first_ref, second_ref), (False, second_ref, first_ref)):

            @pl.when(even == parity)
            def _():
                act(
                    pltpu.make_async_copy(up, next_ref, up_sem),
                    pltpu.make_async_copy(
                        down.at[pl.ds(0, split)], before_ref.at[pl.ds(0, split)], down_sems.at[0]
                    ),
                    pltpu.make_async_copy(
                        down.at[pl.ds(split, down.shape[0] - split)],
                        before_ref.at[pl.ds(split, down.shape[0] - split)],
                        down_sems.at[1],
                    ),
                )

    def right_self(c):
        right_product = product_nt(inverse[c], coupling[...]).astype(jnp.bfloat16)
        return product(coupling[...], right_product).astype(jnp.bfloat16)

    copies[0].wait()
    copies[1].wait()
    real = right_self(0)
    pack_planes(down, [real], 0)
    copies[2].wait()
    pack_planes(up, [inverse[0], inverse[1]], 0)
    pack_tails(up, [inverse[0], inverse[1]])
    on_parity(lambda whole, head, tail: (whole.start(), head.start()))
    imag = right_self(1)
    pack_planes(down, [imag], 1)
    pack_tails(down, [real, imag])
    on_parity(lambda whole, head, tail: tail.start())
    on_parity(lambda whole, head, tail: (whole.wait(), head.wait(), tail.wait()))


def group_iotas():
    sublane = lax.broadcasted_iota(jnp.int32, (SUBLANES, LANES), 0)
    lane = lax.broadcasted_iota(jnp.int32, (SUBLANES, LANES), 1)
    return sublane, lane


def along_lanes(values, lanes):
    return jnp.take_along_axis(values, lanes, axis=1, mode="promise_in_bounds")


def along_lanes_of_halves(values, lanes):
    return lax.gather(
        values,
        lanes[..., None],
        lax.GatherDimensionNumbers(
            offset_dims=(),
            collapsed_slice_dims=(1,),
            start_index_map=(1,),
            operand_batching_dims=(0,),
            start_indices_batching_dims=(0,),
        ),
        slice_sizes=(1, 1),
        mode=lax.GatherScatterMode.PROMISE_IN_BOUNDS,
    )


def table_kernel(
    width, neighbors_ref, phonon_ref, lead_ref, coupling_ref,
    columns_ref, slots_ref, samples_ref, lead_held, coupling_held,
    wide, flat, samples, sems,
):
    fetches = [
        pltpu.make_async_copy(source, held, sems.at[i])
        for i, (source, held) in enumerate(
            ((coupling_ref, coupling_held), (lead_ref, lead_held))
        )
    ]
    for fetch in fetches:
        fetch.start()
    orbitals = neighbors_ref.shape[1]
    groups = orbitals // SUBLANES
    energies = phonon_ref.shape[0]
    sublane, lane = group_iotas()
    own = sublane == lane // width
    wide[...] = jnp.zeros(wide.shape, wide.dtype)
    wide[:, :width] = neighbors_ref[0]
    flat[...] = jnp.full(flat.shape, -1.0, flat.dtype)
    samples[...] = jnp.zeros(samples.shape, samples.dtype)
    tiles = slots_ref.shape[1] // LANES
    for r in range(groups):
        rows = slice(r * SUBLANES, (r + 1) * SUBLANES)
        group = wide[rows, :]
        columns = along_lanes(group, lane % width)
        columns_ref[rows, :] = columns
        flat[r : r + 1, :] = jnp.sum(
            jnp.where(own, columns.astype(jnp.float32), 0.0), axis=0, keepdims=True
        )
        found = [jnp.full((SUBLANES, LANES), -1, jnp.int32) for _ in range(tiles)]
        for k in range(width):
            column = jnp.broadcast_to(group[:, k : k + 1], (SUBLANES, LANES))
            slot = sublane * width + k
            for t in range(tiles):
                found[t] = jnp.where(column == lane + t * LANES, slot, found[t])
        if r % 2 == 1:
            both = slice((r - 1) * SUBLANES, (r + 1) * SUBLANES)
            for t in range(tiles):
                slots_ref[both, t * LANES : (t + 1) * LANES] = jnp.concatenate(
                    [found_before[t], found[t]], axis=0
                ).astype(jnp.int16)
        found_before = found
        for e in range(energies):
            samples[e, :, r, :] = phonon_ref[e, 0, :, r * LANES : (r + 1) * LANES].astype(
                jnp.float32
            )
    for r in range(flat.shape[0] // SUBLANES):
        rows = slice(r * SUBLANES, (r + 1) * SUBLANES)
        here = flat[rows, :]
        values = [[samples[e, c, rows, :] for c in range(2)] for e in range(energies)]
        totals = [list(pair) for pair in values]
        for d in range(1, width):
            turned = (lane // width) * width + (lane + d) % width
            same = here == along_lanes(here, turned)
            for e in range(energies):
                for c in range(2):
                    totals[e][c] = totals[e][c] + jnp.where(
                        same, along_lanes(values[e][c], turned), 0.0
                    )
        for e in range(energies):
            for c in range(2):
                samples[e, c, rows, :] = totals[e][c]
    samples_ref[...] = samples[...].astype(jnp.bfloat16)
    for fetch in fetches:
        fetch.wait()


def unpack_kernel(packed_ref, plane_ref):
    unpack_planes(packed_ref, plane_ref)


def green_kernel(
    width, second_ref, first_planes, lead_ref, inverse_ref, coupling_ref, columns_ref,
    green_ref, pair_ref, previous, right_self, wide, flat,
):
    orbitals = inverse_ref.shape[1]
    domain = lax.axis_index("domain")
    even = domain % 2 == 0

    @pl.when(domain == 0)
    def _():
        previous[...] = lead_ref[0]

    @pl.when(even & (domain > 0))
    def _():
        unpack_planes(second_ref, previous)

    @pl.when(even)
    def _():
        right_self[...] = first_planes[...]

    @pl.when(jnp.logical_not(even))
    def _():
        previous[...] = first_planes[...]
        unpack_planes(second_ref, right_self)

    coupling = coupling_ref[0]
    coupled = []
    for c in range(2):
        left_product = product(previous[c], coupling).astype(jnp.bfloat16)
        left_self = product_tn(coupling, left_product).astype(jnp.bfloat16)
        coupled.append(
            (left_self.astype(jnp.float32) + right_self[c].astype(jnp.float32)).astype(jnp.bfloat16)
        )
    own = [inverse_ref[c] for c in range(2)]
    inner = [part.astype(jnp.bfloat16) for part in complex_product(coupled, own)]
    for c, part in enumerate(complex_product(own, inner)):
        green = (own[c].astype(jnp.float32) + part).astype(jnp.bfloat16)
        green_ref[c] = green
        wide[c, :, :orbitals] = green.astype(jnp.float32)
    gather_pairs(width, wide, columns_ref, flat, pair_ref, 0)


def sides_kernel(
    inverses_ref, second_ref, coupling_ref, before_ref, after_ref, inverse_ref, first_inverse, packed, sems
):
    last = inverses_ref.shape[0] - 1
    copies = [
        pltpu.make_async_copy(inverses_ref.at[e, 0, c], held.at[c], sems.at[k, c])
        for k, (e, held) in enumerate(((last, inverse_ref), (0, first_inverse)))
        for c in range(2)
    ]
    copies.append(pltpu.make_async_copy(second_ref, packed, sems.at[2, 0]))
    for copy in copies:
        copy.start()
    coupling = coupling_ref[0]
    for c in range(2):
        copies[c].wait()
        before_ref[c] = product_nt(inverse_ref[c], coupling).astype(jnp.bfloat16)
        after_ref[c] = product(coupling, inverse_ref[c]).astype(jnp.bfloat16)
    for copy in copies[2:]:
        copy.wait()


def add_side(left, value, middle, right):
    inner = complex_product([middle[c] for c in range(2)], [right[c] for c in range(2)])
    outer = complex_product(
        [left[c] for c in range(2)], [part.astype(jnp.bfloat16) for part in inner]
    )
    return [value[c].astype(jnp.float32) + outer[c] for c in range(2)]


def early_kernel(
    first_ref, lead_ref, before_ref, after_ref, inverse_ref, sum_ref, first_planes
):
    domain = lax.axis_index("domain")
    none = (domain % 2 == 1) & (domain == lax.axis_size("domain") - 1)

    @pl.when((domain > 0) & jnp.logical_not(none))
    def _():
        unpack_planes(first_ref, first_planes)

    def write(values):
        for c in range(2):
            sum_ref[c] = values[c]

    @pl.when(domain == 0)
    def _():
        lead = lead_ref[lead_ref.shape[0] - 1]
        write(add_side(before_ref, inverse_ref, lead, after_ref))

    @pl.when((domain % 2 == 1) & jnp.logical_not(none))
    def _():
        write(add_side(before_ref, inverse_ref, first_planes, after_ref))

    @pl.when((domain % 2 == 0) & (domain > 0))
    def _():
        write(add_side(inverse_ref, inverse_ref, first_planes, inverse_ref))

    @pl.when(none)
    def _():
        write([inverse_ref[c].astype(jnp.float32) for c in range(2)])


def late_kernel(
    width, second_ref, first_ref, before_ref, after_ref, inverse_ref, sum_ref, columns_ref, pair_before,
    green_ref, pair_ref, middle, wide, flat,
):
    orbitals = inverse_ref.shape[1]
    domain = lax.axis_index("domain")
    ends = (domain == 0) | ((domain % 2 == 1) & (domain == lax.axis_size("domain") - 1))

    @pl.when(ends)
    def _():
        unpack_planes(first_ref, middle)

    @pl.when(jnp.logical_not(ends))
    def _():
        unpack_planes(second_ref, middle)

    from_before = (domain > 0) & ((domain % 2 == 0) | ends)

    def write(values):
        for c in range(2):
            green = values[c].astype(jnp.bfloat16)
            green_ref[c] = green
            wide[c, :, :orbitals] = green.astype(jnp.float32)

    @pl.when(from_before)
    def _():
        write(add_side(before_ref, sum_ref, middle, after_ref))

    @pl.when(jnp.logical_not(from_before))
    def _():
        write(add_side(inverse_ref, sum_ref, middle, inverse_ref))

    pair_ref[0] = pair_before[0]
    gather_pairs(width, wide, columns_ref, flat, pair_ref, 1)


def gather_pairs(width, wide, columns_ref, flat, pair_ref, place):
    orbitals = columns_ref.shape[0]
    tiles = wide.shape[2] // LANES
    sublane, lane = group_iotas()
    own = sublane == lane // width
    flat[...] = jnp.zeros(flat.shape, flat.dtype)
    for r in range(orbitals // SUBLANES):
        rows = slice(r * SUBLANES, (r + 1) * SUBLANES)
        columns = columns_ref[rows, :]
        within = columns & (LANES - 1)
        tile = columns // LANES
        for c in range(2):
            taken = jnp.zeros((SUBLANES, LANES), jnp.float32)
            for t in range(tiles):
                candidate = along_lanes(wide[c, rows, t * LANES : (t + 1) * LANES], within)
                taken = jnp.where(own & (tile == t), candidate, taken)
            flat[c, r : r + 1, :] = jnp.sum(taken, axis=0, keepdims=True)
    pair_ref[place] = flat[...].astype(jnp.bfloat16)


def group_kernel(shifts_ref, samples_ref, grouped_ref):
    reach = grouped_ref.shape[0] // 2
    grouped_ref[...] = jnp.zeros(grouped_ref.shape, grouped_ref.dtype)

    def add_point(w, carry):
        place = jnp.clip(shifts_ref[w] + reach, 0, 2 * reach)
        for c in range(2):
            grouped_ref[place, c] = grouped_ref[place, c] + samples_ref[w, c].astype(jnp.float32)
        return carry

    lax.fori_loop(0, samples_ref.shape[0], add_point, 0)


def final_kernel(grouped_ref, slots_ref, green_even_ref, green_odd_ref, *rest):
    *pairs, out_ref, sources, merged, self_block, result, sems = rest
    points = sources.shape[0]
    reach = grouped_ref.shape[0] // 2
    orbitals = result.shape[2]
    groups = orbitals // SUBLANES
    tiles = slots_ref.shape[1] // LANES
    used = merged.shape[2]
    me = lax.axis_index("energy")
    if len(pairs) == 1:

        def widen(p, carry):
            for c in range(2):
                sources[p, c] = pairs[0][p, c].astype(jnp.float32)
            return carry

        lax.fori_loop(0, points, widen, 0, unroll=4)
    else:
        for k, array in enumerate(pairs):
            owner = (me ^ NEAR[k // 2 % 3]) ^ (k % 2)
            for e in range(2):
                for c in range(2):
                    sources[2 * owner + e, c] = array[e, c].astype(jnp.float32)

    def add_shift(place, sums):
        sample = [grouped_ref[place, c, :used, :] for c in range(2)]
        after = []
        for e in range(2):
            source = 2 * me + e + reach - place
            keep = jnp.where((source >= 0) & (source < points), 1.0, 0.0)
            source = jnp.clip(source, 0, points - 1)
            real, imag = (sources[source, c, :used, :] for c in range(2))
            after.append(
                (
                    sums[e][0] + keep * (sample[0] * real - sample[1] * imag),
                    sums[e][1] + keep * (sample[0] * imag + sample[1] * real),
                )
            )
        return tuple(after)

    zero = jnp.zeros((used, LANES), jnp.float32)
    sums = lax.fori_loop(0, 2 * reach + 1, add_shift, ((zero, zero), (zero, zero)), unroll=3)
    for e in range(2):
        for c in range(2):
            merged[e, c] = sums[e][c]
    copies = []
    for e, green_ref in enumerate((green_even_ref, green_odd_ref)):
        for q in range(groups // 2):
            both = slice(q * 16, (q + 1) * 16)
            held = [
                jnp.concatenate(
                    [
                        jnp.broadcast_to(merged[e, c, r : r + 1, :], (SUBLANES, LANES))
                        for r in (2 * q, 2 * q + 1)
                    ],
                    axis=0,
                ).astype(jnp.bfloat16)
                for c in range(2)
            ]
            for t in range(tiles):
                columns = slice(t * LANES, (t + 1) * LANES)
                slot = slots_ref[both, columns]
                within = slot & jnp.int16(LANES - 1)
                for c in range(2):
                    self_block[e, c, both, columns] = jnp.where(
                        slot >= 0, along_lanes_of_halves(held[c], within), jnp.bfloat16(0)
                    )
    for e, green_ref in enumerate((green_even_ref, green_odd_ref)):
        green = [green_ref[c] for c in range(2)]
        sigma = [self_block[e, c, :, :orbitals] for c in range(2)]
        scattered = [part.astype(jnp.bfloat16) for part in complex_product(green, sigma)]
        reals = product(scattered[0], green[0])
        imags = product(scattered[1], green[1])

        def put(c, part):
            result[e, c] = (green[c].astype(jnp.float32) + part).astype(jnp.bfloat16)
            copies.append(pltpu.make_async_copy(result.at[e, c], out_ref.at[e, 0, c], sems.at[e, c]))
            copies[-1].start()

        put(0, reals - imags)
        put(1, product(scattered[0] + scattered[1], green[0] + green[1]) - reals - imags)
    for copy in copies:
        copy.wait()


IN_VMEM = pl.BlockSpec(memory_space=pltpu.VMEM)
IN_SMEM = pl.BlockSpec(memory_space=pltpu.SMEM)
IN_HBM = pl.BlockSpec(memory_space=pltpu.HBM)


def call(kernel, out_shape, in_specs, scratch=(), flops=0, bytes_accessed=1 << 20, out_spec=None, limit=4):
    return pl.pallas_call(
        kernel,
        out_shape=out_shape,
        in_specs=in_specs,
        out_specs=out_spec or (IN_VMEM if not isinstance(out_shape, tuple) else (IN_VMEM,) * len(out_shape)),
        scratch_shapes=list(scratch),
        compiler_params=pltpu.CompilerParams(vmem_limit_bytes=limit * MIB),
        cost_estimate=pl.CostEstimate(flops=flops, bytes_accessed=bytes_accessed, transcendentals=0),
    )


def body(inverses, coupling, lead_green, phonon, neighbors, shifts):
    energies = inverses.shape[0]
    orbitals = inverses.shape[3]
    width = neighbors.shape[2]
    points = shifts.shape[0]
    rows = packed_rows(orbitals)
    groups = orbitals * width // LANES
    used = -(-groups // SUBLANES) * SUBLANES
    height = -(-groups // 16) * 16
    padded = -(-orbitals // LANES) * LANES
    bf16, f32 = jnp.bfloat16, jnp.float32
    shape = jax.ShapeDtypeStruct
    cube = 2 * orbitals**3
    plane = (orbitals, orbitals)
    domains = lax.axis_size("domain")
    routes = [
        [swap for i in range(start, domains - 1, 2) for swap in ((i, i + 1), (i + 1, i))]
        for start in range(2)
    ]

    in_hbm = [
        pltpu.with_memory_space_constraint(array, pltpu.HBM)
        for array in (inverses, coupling, lead_green)
    ]

    barred = in_hbm[0]
    received = []
    for e in range(energies):
        sent = call(
            functools.partial(send_kernel, e),
            (shape((rows, LANES), bf16), shape((rows, LANES), bf16)),
            [IN_HBM] * 2,
            [
                pltpu.VMEM((2, *plane), bf16),
                pltpu.VMEM(plane, bf16),
                pltpu.VMEM((rows, LANES), bf16),
                pltpu.VMEM((rows, LANES), bf16),
                pltpu.SemaphoreType.DMA((3,)),
                pltpu.SemaphoreType.DMA,
                pltpu.SemaphoreType.DMA((2,)),
            ],
            flops=4 * cube,
            out_spec=(IN_HBM,) * 2,
        )(barred, in_hbm[1])
        received.append([lax.ppermute(x, "domain", route) for x, route in zip(sent, routes)])
        barred, neighbors, _ = lax.optimization_barrier((barred, neighbors, sent[0]))
        barred = pltpu.with_memory_space_constraint(barred, pltpu.HBM)
    columns, slots, samples, lead, coupling = call(
        functools.partial(table_kernel, width),
        (
            shape((orbitals, LANES), jnp.int32),
            shape((orbitals, padded), jnp.int16),
            shape((energies, 2, height, LANES), bf16),
            pltpu.VMEM(lead_green.shape, bf16),
            pltpu.VMEM(coupling.shape, bf16),
        ),
        [IN_VMEM, IN_VMEM, IN_HBM, IN_HBM],
        [
            pltpu.VMEM((orbitals, LANES), jnp.int32),
            pltpu.VMEM((height, LANES), f32),
            pltpu.VMEM((energies, 2, height, LANES), f32),
            pltpu.SemaphoreType.DMA((2,)),
        ],
        flops=4 * cube,
    )(neighbors, phonon, in_hbm[2], in_hbm[1])
    samples = lax.all_gather(samples, "energy", axis=0, tiled=True)
    columns, samples = lax.optimization_barrier((columns, samples))

    pair_shape = (1, 2, height, LANES)
    block = shape((2, *plane), bf16)

    def unpacked(first):
        return call(unpack_kernel, block, [IN_VMEM])(first)

    first, second = received[0]
    first, second = lax.optimization_barrier((unpacked(first), second))
    before, after, inverse, first_inverse, second = call(
        sides_kernel,
        (*(block,) * 4, shape((rows, LANES), bf16)),
        [IN_HBM, IN_HBM, IN_VMEM],
        [pltpu.SemaphoreType.DMA((3, 2))],
        flops=4 * cube,
    )(in_hbm[0], pltpu.with_memory_space_constraint(second, pltpu.HBM), coupling)
    green_even, pair = call(
        functools.partial(green_kernel, width),
        (block, shape(pair_shape, bf16)),
        [IN_VMEM] * 6,
        [
            pltpu.VMEM((2, *plane), bf16),
            pltpu.VMEM((2, *plane), bf16),
            pltpu.VMEM((2, orbitals, padded), f32),
            pltpu.VMEM((2, height, LANES), f32),
        ],
        flops=12 * cube,
        limit=12,
    )(second, first, lead, first_inverse, coupling, columns)

    reach = points // 4
    grouped = call(
        group_kernel, shape((2 * reach + 1, 2, height, LANES), f32), [IN_SMEM, IN_VMEM]
    )(shifts, samples)

    first, second = received[1]
    first, pair, grouped = lax.optimization_barrier((first, pair, grouped))
    partial_sum = call(
        early_kernel,
        shape((2, *plane), f32),
        [IN_VMEM] * 5,
        [pltpu.VMEM((2, *plane), bf16)],
        flops=6 * cube,
        limit=12,
    )(first, lead, before, after, inverse)
    green_odd, pair = call(
        functools.partial(late_kernel, width),
        (block, shape((2, *pair_shape[1:]), bf16)),
        [IN_VMEM] * 8,
        [
            pltpu.VMEM((2, *plane), bf16),
            pltpu.VMEM((2, orbitals, padded), f32),
            pltpu.VMEM((2, height, LANES), f32),
        ],
        flops=6 * cube,
        limit=12,
    )(second, first, before, after, inverse, partial_sum, columns, pair)
    devices = lax.axis_size("energy")
    if devices == 8 and energies == 2:
        swap = [(i, i ^ 1) for i in range(devices)]
        beside = lax.ppermute(pair, "energy", [(i, i ^ 2) for i in range(devices)])
        across = lax.ppermute(pair, "energy", [(i, i ^ 6) for i in range(2, 6)])
        sources = []
        for array in (pair, across, beside):
            sources += [array, lax.ppermute(array, "energy", swap)]
    else:
        sources = [lax.all_gather(pair, "energy", axis=0, tiled=True)]

    return call(
        final_kernel,
        shape((energies, 1, 2, *plane), bf16),
        [IN_VMEM] * (4 + len(sources)),
        [
            pltpu.VMEM((points, 2, height, LANES), f32),
            pltpu.VMEM((2, 2, used, LANES), f32),
            pltpu.VMEM((2, 2, orbitals, padded), bf16),
            pltpu.VMEM((2, 2, *plane), bf16),
            pltpu.SemaphoreType.DMA((2, 2)),
        ],
        flops=16 * cube,
        out_spec=IN_HBM,
        limit=16,
    )(grouped, slots, green_even, green_odd, *sources)


def solution(mesh):
    return jax.shard_map(
        body,
        mesh=mesh,
        in_specs=(
            P("energy", "domain", None, None, None),
            P("domain", None, None),
            P("energy", None, None, None),
            P("energy", "domain", None, None),
            P("domain", None, None),
            P(),
        ),
        out_specs=P("energy", "domain", None, None, None),
        check_vma=False,
    )
```

```python
import functools

import jax
import jax.numpy as jnp
from jax import lax
from jax.experimental import pallas as pl
from jax.experimental.pallas import tpu as pltpu
from jax.sharding import PartitionSpec as P

LANES = 128
NEAR = (0, 6, 2)
SUBLANES = 8
MIB = 1024 * 1024


def product(first, second):
    return jnp.dot(first, second, preferred_element_type=jnp.float32)


def product_nt(first, second):
    return lax.dot_general(
        first, second, (((1,), (1,)), ((), ())), preferred_element_type=jnp.float32
    )


def product_tn(first, second):
    return lax.dot_general(
        first, second, (((0,), (0,)), ((), ())), preferred_element_type=jnp.float32
    )


def complex_product(first, second):
    reals = product(first[0], second[0])
    imags = product(first[1], second[1])
    both = product(first[0] + first[1], second[0] + second[1])
    return reals - imags, both - reals - imags


def packed_rows(orbitals):
    return 2 * orbitals * orbitals // LANES


def pack_planes(out_ref, planes, place):
    orbitals = planes[0].shape[0]
    whole = orbitals // LANES
    for c, plane in enumerate(planes, place):
        for t in range(whole):
            out_ref[pl.ds((c * whole + t) * orbitals, orbitals), :] = plane[
                :, t * LANES : (t + 1) * LANES
            ]


def pack_tails(out_ref, planes):
    orbitals = planes[0].shape[0]
    whole = orbitals // LANES
    rest = orbitals - whole * LANES
    pieces = LANES // rest // 2
    height = orbitals // pieces
    tails = [
        plane[h * height : (h + 1) * height, whole * LANES :]
        for plane in planes
        for h in range(pieces)
    ]
    out_ref[pl.ds(2 * whole * orbitals, height), :] = jnp.concatenate(tails, axis=1)


def unpack_planes(packed_ref, plane_ref):
    orbitals = plane_ref.shape[1]
    whole = orbitals // LANES
    rest = orbitals - whole * LANES
    pieces = LANES // rest // 2
    height = orbitals // pieces
    tails = packed_ref[pl.ds(2 * whole * orbitals, height), :]
    for c in range(2):
        for t in range(whole):
            plane_ref[c, :, t * LANES : (t + 1) * LANES] = packed_ref[
                pl.ds((c * whole + t) * orbitals, orbitals), :
            ]
        for h in range(pieces):
            start = (c * pieces + h) * rest
            plane_ref[c, h * height : (h + 1) * height, whole * LANES :] = tails[
                :, start : start + rest
            ]


def send_kernel(
    e, inverses_ref, coupling_ref, first_ref, second_ref,
    inverse, coupling, up, down, sems, up_sem, down_sems,
):
    copies = [pltpu.make_async_copy(coupling_ref.at[0], coupling, sems.at[2])]
    for c in range(2):
        copies.append(pltpu.make_async_copy(inverses_ref.at[e, 0, c], inverse.at[c], sems.at[c]))
    for copy in copies:
        copy.start()
    even = lax.axis_index("domain") % 2 == 0
    split = inverse.shape[1] * (inverse.shape[2] // LANES)

    def on_parity(act):
        for parity, next_ref, before_ref in ((True, first_ref, second_ref), (False, second_ref, first_ref)):

            @pl.when(even == parity)
            def _():
                act(
                    pltpu.make_async_copy(up, next_ref, up_sem),
                    pltpu.make_async_copy(
                        down.at[pl.ds(0, split)], before_ref.at[pl.ds(0, split)], down_sems.at[0]
                    ),
                    pltpu.make_async_copy(
                        down.at[pl.ds(split, down.shape[0] - split)],
                        before_ref.at[pl.ds(split, down.shape[0] - split)],
                        down_sems.at[1],
                    ),
                )

    def right_self(c):
        right_product = product_nt(inverse[c], coupling[...]).astype(jnp.bfloat16)
        return product(coupling[...], right_product).astype(jnp.bfloat16)

    copies[0].wait()
    copies[1].wait()
    real = right_self(0)
    pack_planes(down, [real], 0)
    copies[2].wait()
    pack_planes(up, [inverse[0], inverse[1]], 0)
    pack_tails(up, [inverse[0], inverse[1]])
    on_parity(lambda whole, head, tail: (whole.start(), head.start()))
    imag = right_self(1)
    pack_planes(down, [imag], 1)
    pack_tails(down, [real, imag])
    on_parity(lambda whole, head, tail: tail.start())
    on_parity(lambda whole, head, tail: (whole.wait(), head.wait(), tail.wait()))


def group_iotas():
    sublane = lax.broadcasted_iota(jnp.int32, (SUBLANES, LANES), 0)
    lane = lax.broadcasted_iota(jnp.int32, (SUBLANES, LANES), 1)
    return sublane, lane


def along_lanes(values, lanes):
    return jnp.take_along_axis(values, lanes, axis=1, mode="promise_in_bounds")


def along_lanes_of_halves(values, lanes):
    return lax.gather(
        values,
        lanes[..., None],
        lax.GatherDimensionNumbers(
            offset_dims=(),
            collapsed_slice_dims=(1,),
            start_index_map=(1,),
            operand_batching_dims=(0,),
            start_indices_batching_dims=(0,),
        ),
        slice_sizes=(1, 1),
        mode=lax.GatherScatterMode.PROMISE_IN_BOUNDS,
    )


def table_kernel(
    width, neighbors_ref, phonon_ref, lead_ref, coupling_ref,
    columns_ref, slots_ref, samples_ref, lead_held, coupling_held,
    wide, flat, samples, sems,
):
    fetches = [
        pltpu.make_async_copy(source, held, sems.at[i])
        for i, (source, held) in enumerate(
            ((coupling_ref, coupling_held), (lead_ref, lead_held))
        )
    ]
    for fetch in fetches:
        fetch.start()
    orbitals = neighbors_ref.shape[1]
    groups = orbitals // SUBLANES
    energies = phonon_ref.shape[0]
    sublane, lane = group_iotas()
    own = sublane == lane // width
    wide[...] = jnp.zeros(wide.shape, wide.dtype)
    wide[:, :width] = neighbors_ref[0]
    flat[...] = jnp.full(flat.shape, -1.0, flat.dtype)
    samples[...] = jnp.zeros(samples.shape, samples.dtype)
    tiles = slots_ref.shape[1] // LANES
    for r in range(groups):
        rows = slice(r * SUBLANES, (r + 1) * SUBLANES)
        group = wide[rows, :]
        columns = along_lanes(group, lane % width)
        flat[r : r + 1, :] = jnp.sum(
            jnp.where(own, columns.astype(jnp.float32), 0.0), axis=0, keepdims=True
        )
        found = [jnp.full((SUBLANES, LANES), -1, jnp.int32) for _ in range(tiles)]
        for k in range(width):
            column = jnp.broadcast_to(group[:, k : k + 1], (SUBLANES, LANES))
            slot = sublane * width + k
            for t in range(tiles):
                found[t] = jnp.where(column == lane + t * LANES, slot, found[t])
        if r % 2 == 1:
            both = slice((r - 1) * SUBLANES, (r + 1) * SUBLANES)
            columns_ref[both, :] = jnp.concatenate([columns_before, columns], axis=0).astype(jnp.int16)
            for t in range(tiles):
                slots_ref[both, t * LANES : (t + 1) * LANES] = jnp.concatenate(
                    [found_before[t], found[t]], axis=0
                ).astype(jnp.int16)
        found_before, columns_before = found, columns
        for e in range(energies):
            samples[e, :, r, :] = phonon_ref[e, 0, :, r * LANES : (r + 1) * LANES].astype(
                jnp.float32
            )
    for r in range(flat.shape[0] // SUBLANES):
        rows = slice(r * SUBLANES, (r + 1) * SUBLANES)
        here = flat[rows, :]
        values = [[samples[e, c, rows, :] for c in range(2)] for e in range(energies)]
        totals = [list(pair) for pair in values]
        for d in range(1, width):
            turned = (lane // width) * width + (lane + d) % width
            same = here == along_lanes(here, turned)
            for e in range(energies):
                for c in range(2):
                    totals[e][c] = totals[e][c] + jnp.where(
                        same, along_lanes(values[e][c], turned), 0.0
                    )
        for e in range(energies):
            for c in range(2):
                samples[e, c, rows, :] = totals[e][c]
    samples_ref[...] = samples[...].astype(jnp.bfloat16)
    for fetch in fetches:
        fetch.wait()


def unpack_kernel(packed_ref, plane_ref):
    unpack_planes(packed_ref, plane_ref)


def green_kernel(
    width, second_ref, first_planes, lead_ref, inverse_ref, coupling_ref, columns_ref,
    green_ref, pair_ref, previous, right_self, wide, flat,
):
    orbitals = inverse_ref.shape[1]
    domain = lax.axis_index("domain")
    even = domain % 2 == 0

    @pl.when(domain == 0)
    def _():
        previous[...] = lead_ref[0]

    @pl.when(even & (domain > 0))
    def _():
        unpack_planes(second_ref, previous)

    @pl.when(even)
    def _():
        right_self[...] = first_planes[...]

    @pl.when(jnp.logical_not(even))
    def _():
        previous[...] = first_planes[...]
        unpack_planes(second_ref, right_self)

    coupling = coupling_ref[0]
    coupled = []
    for c in range(2):
        left_product = product(previous[c], coupling).astype(jnp.bfloat16)
        left_self = product_tn(coupling, left_product).astype(jnp.bfloat16)
        coupled.append(
            (left_self.astype(jnp.float32) + right_self[c].astype(jnp.float32)).astype(jnp.bfloat16)
        )
    own = [inverse_ref[c] for c in range(2)]
    inner = [part.astype(jnp.bfloat16) for part in complex_product(coupled, own)]
    for c, part in enumerate(complex_product(own, inner)):
        green = (own[c].astype(jnp.float32) + part).astype(jnp.bfloat16)
        green_ref[c] = green
        wide[c, :, :orbitals] = green
    gather_pairs(width, wide, columns_ref, flat, pair_ref, 0)


def sides_kernel(
    inverses_ref, second_ref, coupling_ref, before_ref, after_ref, inverse_ref, first_inverse, packed, sems
):
    last = inverses_ref.shape[0] - 1
    copies = [
        pltpu.make_async_copy(inverses_ref.at[e, 0, c], held.at[c], sems.at[k, c])
        for k, (e, held) in enumerate(((last, inverse_ref), (0, first_inverse)))
        for c in range(2)
    ]
    copies.append(pltpu.make_async_copy(second_ref, packed, sems.at[2, 0]))
    for copy in copies:
        copy.start()
    coupling = coupling_ref[0]
    for c in range(2):
        copies[c].wait()
        before_ref[c] = product_nt(inverse_ref[c], coupling).astype(jnp.bfloat16)
        after_ref[c] = product(coupling, inverse_ref[c]).astype(jnp.bfloat16)
    for copy in copies[2:]:
        copy.wait()


def add_side(left, value, middle, right):
    inner = complex_product([middle[c] for c in range(2)], [right[c] for c in range(2)])
    outer = complex_product(
        [left[c] for c in range(2)], [part.astype(jnp.bfloat16) for part in inner]
    )
    return [value[c].astype(jnp.float32) + outer[c] for c in range(2)]


def early_kernel(
    first_ref, lead_ref, before_ref, after_ref, inverse_ref, sum_ref, first_planes
):
    domain = lax.axis_index("domain")
    none = (domain % 2 == 1) & (domain == lax.axis_size("domain") - 1)

    @pl.when((domain > 0) & jnp.logical_not(none))
    def _():
        unpack_planes(first_ref, first_planes)

    def write(values):
        for c in range(2):
            sum_ref[c] = values[c]

    @pl.when(domain == 0)
    def _():
        lead = lead_ref[lead_ref.shape[0] - 1]
        write(add_side(before_ref, inverse_ref, lead, after_ref))

    @pl.when((domain % 2 == 1) & jnp.logical_not(none))
    def _():
        write(add_side(before_ref, inverse_ref, first_planes, after_ref))

    @pl.when((domain % 2 == 0) & (domain > 0))
    def _():
        write(add_side(inverse_ref, inverse_ref, first_planes, inverse_ref))

    @pl.when(none)
    def _():
        write([inverse_ref[c].astype(jnp.float32) for c in range(2)])


def late_kernel(
    width, second_ref, first_ref, before_ref, after_ref, inverse_ref, sum_ref, columns_ref, pair_before,
    green_ref, pair_ref, middle, wide, flat,
):
    orbitals = inverse_ref.shape[1]
    domain = lax.axis_index("domain")
    ends = (domain == 0) | ((domain % 2 == 1) & (domain == lax.axis_size("domain") - 1))

    @pl.when(ends)
    def _():
        unpack_planes(first_ref, middle)

    @pl.when(jnp.logical_not(ends))
    def _():
        unpack_planes(second_ref, middle)

    from_before = (domain > 0) & ((domain % 2 == 0) | ends)

    def write(values):
        for c in range(2):
            green = values[c].astype(jnp.bfloat16)
            green_ref[c] = green
            wide[c, :, :orbitals] = green

    @pl.when(from_before)
    def _():
        write(add_side(before_ref, sum_ref, middle, after_ref))

    @pl.when(jnp.logical_not(from_before))
    def _():
        write(add_side(inverse_ref, sum_ref, middle, inverse_ref))

    pair_ref[0] = pair_before[0]
    gather_pairs(width, wide, columns_ref, flat, pair_ref, 1)


def gather_pairs(width, wide, columns_ref, flat, pair_ref, place):
    orbitals = columns_ref.shape[0]
    tiles = wide.shape[2] // LANES
    sublane, lane = group_iotas()
    own = sublane == lane // width
    flat[...] = jnp.zeros(flat.shape, flat.dtype)
    for q in range(orbitals // 16):
        both = slice(q * 16, (q + 1) * 16)
        columns = columns_ref[both, :]
        within = columns & jnp.int16(LANES - 1)
        for c in range(2):
            taken = along_lanes_of_halves(wide[c, both, :LANES], within)
            for t in range(1, tiles):
                candidate = along_lanes_of_halves(wide[c, both, t * LANES : (t + 1) * LANES], within)
                taken = jnp.where(columns >= jnp.int16(t * LANES), candidate, taken)
            values = taken.astype(jnp.float32)
            for k in range(2):
                half = jnp.where(own, values[k * SUBLANES : (k + 1) * SUBLANES], 0.0)
                flat[c, 2 * q + k : 2 * q + k + 1, :] = jnp.sum(half, axis=0, keepdims=True)
    pair_ref[place] = flat[...].astype(jnp.bfloat16)


def group_kernel(shifts_ref, samples_ref, grouped_ref):
    reach = grouped_ref.shape[0] // 2
    grouped_ref[...] = jnp.zeros(grouped_ref.shape, grouped_ref.dtype)

    def add_point(w, carry):
        place = jnp.clip(shifts_ref[w] + reach, 0, 2 * reach)
        for c in range(2):
            grouped_ref[place, c] = grouped_ref[place, c] + samples_ref[w, c].astype(jnp.float32)
        return carry

    lax.fori_loop(0, samples_ref.shape[0], add_point, 0)


def final_kernel(grouped_ref, slots_ref, green_even_ref, green_odd_ref, *rest):
    *pairs, out_ref, sources, merged, self_block, result, sems = rest
    points = sources.shape[0]
    reach = grouped_ref.shape[0] // 2
    orbitals = result.shape[2]
    groups = orbitals // SUBLANES
    tiles = slots_ref.shape[1] // LANES
    used = merged.shape[2]
    me = lax.axis_index("energy")
    if len(pairs) == 1:

        def widen(p, carry):
            for c in range(2):
                sources[p, c] = pairs[0][p, c].astype(jnp.float32)
            return carry

        lax.fori_loop(0, points, widen, 0, unroll=4)
    else:
        for k, array in enumerate(pairs):
            owner = (me ^ NEAR[k // 2 % 3]) ^ (k % 2)
            for e in range(2):
                for c in range(2):
                    sources[2 * owner + e, c] = array[e, c].astype(jnp.float32)

    def add_shift(place, sums):
        sample = [grouped_ref[place, c, :used, :] for c in range(2)]
        after = []
        for e in range(2):
            source = 2 * me + e + reach - place
            keep = jnp.where((source >= 0) & (source < points), 1.0, 0.0)
            source = jnp.clip(source, 0, points - 1)
            real, imag = (sources[source, c, :used, :] for c in range(2))
            after.append(
                (
                    sums[e][0] + keep * (sample[0] * real - sample[1] * imag),
                    sums[e][1] + keep * (sample[0] * imag + sample[1] * real),
                )
            )
        return tuple(after)

    zero = jnp.zeros((used, LANES), jnp.float32)
    sums = lax.fori_loop(0, 2 * reach + 1, add_shift, ((zero, zero), (zero, zero)), unroll=3)
    for e in range(2):
        for c in range(2):
            merged[e, c] = sums[e][c]
    copies = []
    for e, green_ref in enumerate((green_even_ref, green_odd_ref)):
        for q in range(groups // 2):
            both = slice(q * 16, (q + 1) * 16)
            held = [
                jnp.concatenate(
                    [
                        jnp.broadcast_to(merged[e, c, r : r + 1, :], (SUBLANES, LANES))
                        for r in (2 * q, 2 * q + 1)
                    ],
                    axis=0,
                ).astype(jnp.bfloat16)
                for c in range(2)
            ]
            for t in range(tiles):
                columns = slice(t * LANES, (t + 1) * LANES)
                slot = slots_ref[both, columns]
                within = slot & jnp.int16(LANES - 1)
                for c in range(2):
                    self_block[e, c, both, columns] = jnp.where(
                        slot >= 0, along_lanes_of_halves(held[c], within), jnp.bfloat16(0)
                    )
    for e, green_ref in enumerate((green_even_ref, green_odd_ref)):
        green = [green_ref[c] for c in range(2)]
        sigma = [self_block[e, c, :, :orbitals] for c in range(2)]
        scattered = [part.astype(jnp.bfloat16) for part in complex_product(green, sigma)]
        reals = product(scattered[0], green[0])
        imags = product(scattered[1], green[1])

        def put(c, part):
            result[e, c] = (green[c].astype(jnp.float32) + part).astype(jnp.bfloat16)
            copies.append(pltpu.make_async_copy(result.at[e, c], out_ref.at[e, 0, c], sems.at[e, c]))
            copies[-1].start()

        put(0, reals - imags)
        put(1, product(scattered[0] + scattered[1], green[0] + green[1]) - reals - imags)
    for copy in copies:
        copy.wait()


IN_VMEM = pl.BlockSpec(memory_space=pltpu.VMEM)
IN_SMEM = pl.BlockSpec(memory_space=pltpu.SMEM)
IN_HBM = pl.BlockSpec(memory_space=pltpu.HBM)


def call(kernel, out_shape, in_specs, scratch=(), flops=0, bytes_accessed=1 << 20, out_spec=None, limit=4):
    return pl.pallas_call(
        kernel,
        out_shape=out_shape,
        in_specs=in_specs,
        out_specs=out_spec or (IN_VMEM if not isinstance(out_shape, tuple) else (IN_VMEM,) * len(out_shape)),
        scratch_shapes=list(scratch),
        compiler_params=pltpu.CompilerParams(vmem_limit_bytes=limit * MIB),
        cost_estimate=pl.CostEstimate(flops=flops, bytes_accessed=bytes_accessed, transcendentals=0),
    )


def body(inverses, coupling, lead_green, phonon, neighbors, shifts):
    energies = inverses.shape[0]
    orbitals = inverses.shape[3]
    width = neighbors.shape[2]
    points = shifts.shape[0]
    rows = packed_rows(orbitals)
    groups = orbitals * width // LANES
    used = -(-groups // SUBLANES) * SUBLANES
    height = -(-groups // 16) * 16
    padded = -(-orbitals // LANES) * LANES
    bf16, f32 = jnp.bfloat16, jnp.float32
    shape = jax.ShapeDtypeStruct
    cube = 2 * orbitals**3
    plane = (orbitals, orbitals)
    domains = lax.axis_size("domain")
    routes = [
        [swap for i in range(start, domains - 1, 2) for swap in ((i, i + 1), (i + 1, i))]
        for start in range(2)
    ]

    in_hbm = [
        pltpu.with_memory_space_constraint(array, pltpu.HBM)
        for array in (inverses, coupling, lead_green)
    ]

    barred = in_hbm[0]
    received = []
    for e in range(energies):
        sent = call(
            functools.partial(send_kernel, e),
            (shape((rows, LANES), bf16), shape((rows, LANES), bf16)),
            [IN_HBM] * 2,
            [
                pltpu.VMEM((2, *plane), bf16),
                pltpu.VMEM(plane, bf16),
                pltpu.VMEM((rows, LANES), bf16),
                pltpu.VMEM((rows, LANES), bf16),
                pltpu.SemaphoreType.DMA((3,)),
                pltpu.SemaphoreType.DMA,
                pltpu.SemaphoreType.DMA((2,)),
            ],
            flops=4 * cube,
            out_spec=(IN_HBM,) * 2,
        )(barred, in_hbm[1])
        received.append([lax.ppermute(x, "domain", route) for x, route in zip(sent, routes)])
        barred, neighbors, _ = lax.optimization_barrier((barred, neighbors, sent[0]))
        barred = pltpu.with_memory_space_constraint(barred, pltpu.HBM)
    columns, slots, samples, lead, coupling = call(
        functools.partial(table_kernel, width),
        (
            shape((orbitals, LANES), jnp.int16),
            shape((orbitals, padded), jnp.int16),
            shape((energies, 2, height, LANES), bf16),
            pltpu.VMEM(lead_green.shape, bf16),
            pltpu.VMEM(coupling.shape, bf16),
        ),
        [IN_VMEM, IN_VMEM, IN_HBM, IN_HBM],
        [
            pltpu.VMEM((orbitals, LANES), jnp.int32),
            pltpu.VMEM((height, LANES), f32),
            pltpu.VMEM((energies, 2, height, LANES), f32),
            pltpu.SemaphoreType.DMA((2,)),
        ],
        flops=4 * cube,
    )(neighbors, phonon, in_hbm[2], in_hbm[1])
    samples = lax.all_gather(samples, "energy", axis=0, tiled=True)
    columns, samples = lax.optimization_barrier((columns, samples))

    pair_shape = (1, 2, height, LANES)
    block = shape((2, *plane), bf16)

    def unpacked(first):
        return call(unpack_kernel, block, [IN_VMEM])(first)

    first, second = received[0]
    first, second = lax.optimization_barrier((unpacked(first), second))
    before, after, inverse, first_inverse, second = call(
        sides_kernel,
        (*(block,) * 4, shape((rows, LANES), bf16)),
        [IN_HBM, IN_HBM, IN_VMEM],
        [pltpu.SemaphoreType.DMA((3, 2))],
        flops=4 * cube,
    )(in_hbm[0], pltpu.with_memory_space_constraint(second, pltpu.HBM), coupling)
    green_even, pair = call(
        functools.partial(green_kernel, width),
        (block, shape(pair_shape, bf16)),
        [IN_VMEM] * 6,
        [
            pltpu.VMEM((2, *plane), bf16),
            pltpu.VMEM((2, *plane), bf16),
            pltpu.VMEM((2, orbitals, padded), bf16),
            pltpu.VMEM((2, height, LANES), f32),
        ],
        flops=12 * cube,
        limit=12,
    )(second, first, lead, first_inverse, coupling, columns)

    reach = points // 4
    grouped = call(
        group_kernel, shape((2 * reach + 1, 2, height, LANES), f32), [IN_SMEM, IN_VMEM]
    )(shifts, samples)

    first, second = received[1]
    first, pair, grouped = lax.optimization_barrier((first, pair, grouped))
    partial_sum = call(
        early_kernel,
        shape((2, *plane), f32),
        [IN_VMEM] * 5,
        [pltpu.VMEM((2, *plane), bf16)],
        flops=6 * cube,
        limit=12,
    )(first, lead, before, after, inverse)
    green_odd, pair = call(
        functools.partial(late_kernel, width),
        (block, shape((2, *pair_shape[1:]), bf16)),
        [IN_VMEM] * 8,
        [
            pltpu.VMEM((2, *plane), bf16),
            pltpu.VMEM((2, orbitals, padded), bf16),
            pltpu.VMEM((2, height, LANES), f32),
        ],
        flops=6 * cube,
        limit=12,
    )(second, first, before, after, inverse, partial_sum, columns, pair)
    devices = lax.axis_size("energy")
    if devices == 8 and energies == 2:
        swap = [(i, i ^ 1) for i in range(devices)]
        beside = lax.ppermute(pair, "energy", [(i, i ^ 2) for i in range(devices)])
        across = lax.ppermute(pair, "energy", [(i, i ^ 6) for i in range(2, 6)])
        sources = []
        for array in (pair, across, beside):
            sources += [array, lax.ppermute(array, "energy", swap)]
    else:
        sources = [lax.all_gather(pair, "energy", axis=0, tiled=True)]

    return call(
        final_kernel,
        shape((energies, 1, 2, *plane), bf16),
        [IN_VMEM] * (4 + len(sources)),
        [
            pltpu.VMEM((points, 2, height, LANES), f32),
            pltpu.VMEM((2, 2, used, LANES), f32),
            pltpu.VMEM((2, 2, orbitals, padded), bf16),
            pltpu.VMEM((2, 2, *plane), bf16),
            pltpu.SemaphoreType.DMA((2, 2)),
        ],
        flops=16 * cube,
        out_spec=IN_HBM,
        limit=16,
    )(grouped, slots, green_even, green_odd, *sources)


def solution(mesh):
    return jax.shard_map(
        body,
        mesh=mesh,
        in_specs=(
            P("energy", "domain", None, None, None),
            P("domain", None, None),
            P("energy", None, None, None),
            P("energy", "domain", None, None),
            P("domain", None, None),
            P(),
        ),
        out_specs=P("energy", "domain", None, None, None),
        check_vma=False,
    )
```
